32 devices in a mesh: dp: 8 (over z, core), tensor: 4 (over y, x).
Axes of the slice: x: 2, y: 2, z: 4, core: 2. Of those that a mesh axis runs over, the one named last changes fastest.
Arguments:
- tokens: bfloat16 [8192, 1536], P(('dp', 'tensor')), may hold values from -6 to 6
- cotangent: bfloat16 [8192, 1536], P(('dp', 'tensor')), may hold values from -6 to 6
- lengths: int32 [8, 4], P('dp'), may hold values from 1 to 512, 1024 in all within a row
- routes: int32 [8192, 8], P('dp'), may hold values from 0 to 39, all different within a row; in each aligned block of 256 rows (0 to 255, 256 to 511, ...) at most 81 rows name the same one
- norm_gains: float32 [2, 1536], replicated, may hold values from 0.5 to 1.5
- router_weight: bfloat16 [1536, 40], replicated, may hold values from -0.078125 to 0.078125
- qkv_weight: bfloat16 [8, 1536, 320], P('tensor', 'dp'), may hold values from -0.15625 to 0.15625
- out_weight: bfloat16 [8, 192, 1536], P('tensor', None, 'dp'), may hold values from -0.4375 to 0.4375
- expert_in: bfloat16 [40, 1536, 1024], P('tensor', 'dp'), may hold values from -0.15625 to 0.15625
- expert_out: bfloat16 [40, 512, 1536], P('tensor', None, 'dp'), may hold values from -1 to 1
Outputs:
- layer_output: bfloat16 [8192, 1536], P(('dp', 'tensor'))
- input_grad: float32 [8192, 1536], P(('dp', 'tensor'))
- norm_gains_grad: float32 [2, 1536], replicated
- router_grad: float32 [1536, 40], replicated
- qkv_grad: float32 [8, 1536, 320], P('tensor', 'dp')
- out_weight_grad: float32 [8, 192, 1536], P('tensor', None, 'dp')
- expert_in_grad: float32 [40, 1536, 1024], P('tensor', 'dp')
- expert_out_grad: float32 [40, 512, 1536], P('tensor', None, 'dp')
The draws below stay inside these ranges and needn't reach their ends.
Inputs may be any that keep to these rules, and one draw needn't show every extreme that they name: `lengths`: each row lists one group's sequences in order; they sum to 1024, and the longest of each row is exactly 512. `routes`: each row names 8 different experts. In every aligned block of 256 rows no expert is named by more than 81 rows, and in some block one expert is named by exactly 81.
All inputs are finite; a program needn't handle non-finite values.
Results may differ from the reference program's by a relative error of at most 0.02.
Values may be sent and summed in bfloat16 or wider, within the bound.
No kernel may reach another device: no remote copies, remote signals or barrier semaphores. Data moves between devices by JAX's collectives and lax.ppermute only.
A program may use at most 448 MiB of HBM per device.

```python
import math
import jax
import jax.numpy as jnp
import numpy as np
from jax import lax

D = 1536
HD = 64
KV = 8
GRP = 3
HQ = 24
F = 512
E = 40
TOP = 8
TOK_DEV = 256
GROUP_TOK = 1024
TOKENS = 8192
SEQ_MAX = 512
SEQS = 4
MOST = 81
N_DP = 8


def levels(rng, shape, split, low, high):
    factor_of = 1.0
    for axis_at, parts in split:
        steps = jax.random.uniform(jax.random.fold_in(jax.random.fold_in(rng, 6), axis_at), (parts,), jnp.float32, low / len(split), high / len(split))
        factor_of = factor_of * jnp.repeat(jnp.exp(steps), shape[axis_at] // parts).reshape((-1,) + (1,) * (len(shape) - 1 - axis_at))
    return factor_of


def length_profile(amount, total, most, slope):
    weights = [(1 << 20) // math.isqrt(grade ** slope) + 1 for grade in range(2, amount + 1)]
    spare, given = total - most - (amount - 1), [1] * (amount - 1)
    while spare > 0:
        movable = [i for i in range(amount - 1) if given[i] < most]
        mass, budget = sum([weights[i] for i in movable]), spare
        for i in movable:
            addition = min(most - given[i], max(1, budget * weights[i] // mass), spare)
            given[i] = given[i] + addition
            spare = spare - addition
    return np.array([most] + given)


def ragged_sizes(stream_key, count, total, bound, skew):
    if count == 2:
        one = jax.random.randint(stream_key, (), max(1, total - bound), min(bound, total - 1) + 1)
        return jnp.stack([one, total - one])
    sizes = jnp.asarray(length_profile(count, total, bound, skew), jnp.int32)
    couples = (count - 1) // 2
    source_of, receiver = sizes[1:1 + 2 * couples:2], sizes[2:2 + 2 * couples:2]
    slack = jnp.minimum(source_of - 1, bound - receiver)
    passed = jax.random.randint(jax.random.fold_in(stream_key, 1), (couples,), 0, 1 << 20) % (slack + 1)
    sizes = sizes.at[1:1 + 2 * couples:2].set(source_of - passed).at[2:2 + 2 * couples:2].set(receiver + passed)
    return sizes[jax.random.permutation(jax.random.fold_in(stream_key, 2), count)]


def deal_out(key, own, number, rows, number_of, top, reach, skew):
    order = jax.random.permutation(key, number_of)
    crowded, common = portions_of(number_of, rows * top, reach, skew, True), portions_of(number_of, rows * top, reach, skew, False)
    places = jnp.arange(number_of)

    def named(sizes, offset_by):
        used = int((sizes > 0).sum())
        fixed = max(1, used // 4)
        shifted = fixed + (places - fixed + offset_by * (used - fixed)) % max(1, number_of - fixed)
        return jnp.zeros((number_of,), jnp.int32).at[order[jnp.where(places < fixed, places, shifted)]].set(jnp.asarray(sizes, jnp.int32))

    sizes = jnp.where(number % 4 == 0, named(crowded, number // 4), named(common, number - number // 4 - 1))
    mixed = jax.random.permutation(jax.random.fold_in(own, 3), number_of)
    source_of, receiver = mixed[0:number_of // 2 * 2:2], mixed[1:number_of // 2 * 2:2]
    slack = jnp.minimum(sizes[source_of] - 1, reach - sizes[receiver]) // 2
    slack = jnp.where((source_of == order[0]) | (receiver == order[0]) | (sizes[receiver] == 0), 0, jnp.maximum(slack, 0))
    shifted = jax.random.randint(jax.random.fold_in(own, 4), (number_of // 2,), 0, 1 << 20) % (slack + 1)
    sizes = sizes.at[source_of].add(-shifted).at[receiver].add(shifted)
    labels = jnp.searchsorted(jnp.cumsum(sizes), jnp.arange(rows * top), side="right").astype(jnp.int32)
    table = labels.reshape(top, rows).T
    table = table[jax.random.permutation(jax.random.fold_in(own, 1), rows)]
    offset_by = jax.random.randint(jax.random.fold_in(own, 2), (rows, 1), 0, top)
    return jnp.take_along_axis(table, (jnp.arange(top)[None, :] + offset_by) % top, axis=1)


def portions_of(amount, total, most, slope, full):
    weights = [(1 << 20) // math.isqrt(grade ** slope) + 1 for grade in range(1, amount + 1)]
    largest = most if full else min(most, max(-(-total // amount), total * weights[0] // sum(weights)))
    least = 1 if total - largest >= amount - 1 else 0
    counts, rest = [largest] + [least] * (amount - 1), total - largest - least * (amount - 1)
    while rest > 0:
        movable = [i for i in range(1, amount) if counts[i] < largest] or [i for i in range(1, amount) if counts[i] < most]
        mass, left = sum([weights[i] for i in movable]), rest
        for i in movable:
            addition = min(most - counts[i], max(1, left * weights[i] // mass), rest)
            counts[i] = counts[i] + addition
            rest = rest - addition
    return np.array(counts)


def centred(stream_key, shape, scale, limit, split=(), held_as=jnp.bfloat16):
    loudness = levels(stream_key, shape, split, -0.22, 0.18) if split else 1.0
    values = jax.random.normal(stream_key, shape, jnp.float32) * scale * loudness
    return jnp.minimum(jnp.maximum(values, -limit), limit).astype(held_as)


def setup_inputs(seed: int = 0) -> dict:
    seeds = jax.random.split(jax.random.key(seed), 11)
    tokens = centred(seeds[0], (TOKENS, D), 1.0, 6.0, ((0, 32),))
    cotangent = centred(seeds[1], (TOKENS, D), 1.0, 6.0, ((0, 32),))
    lengths = jax.vmap(lambda own: ragged_sizes(own, SEQS, GROUP_TOK, SEQ_MAX, 2))(jax.random.split(seeds[2], N_DP)).reshape((N_DP, SEQS)).astype(jnp.int32)
    routes_keys = jax.random.split(jax.random.fold_in(seeds[3], 1), TOKENS // TOK_DEV)
    routes_turns = jax.random.permutation(jax.random.fold_in(seeds[3], 3), TOKENS // TOK_DEV)
    routes = jax.vmap(lambda own, number: deal_out(jax.random.fold_in(seeds[3], 2), own, number, TOK_DEV, E, TOP, MOST, 1))(routes_keys, routes_turns).reshape((TOKENS, TOP))
    norm_gains = jnp.clip(1.0 + 0.1 * jax.random.normal(seeds[4], (2, D), jnp.float32), 0.5, 1.5)
    router_weight = centred(seeds[5], (D, E), (4 * D) ** -0.5, 0.078125)
    qkv_weight = centred(seeds[6], (KV, D, (GRP + 2) * HD), D ** -0.5, 0.15625, ((0, 4), (1, 8)))
    out_weight = centred(seeds[7], (KV, GRP * HD, D), (HQ * HD // 8) ** -0.5, 0.4375, ((0, 4), (2, 8)))
    expert_in = centred(seeds[8], (E, D, 2 * F), D ** -0.5, 0.15625, ((0, 4), (1, 8)))
    expert_out = centred(seeds[9], (E, F, D), (F // 16) ** -0.5, 1.0, ((0, 4), (2, 8)))
    return {"tokens": tokens, "cotangent": cotangent, "lengths": lengths, "routes": routes, "norm_gains": norm_gains, "router_weight": router_weight, "qkv_weight": qkv_weight, "out_weight": out_weight, "expert_in": expert_in, "expert_out": expert_out}


@jax.custom_vjp
def low(v):
    return lax.optimization_barrier(v.astype(jnp.bfloat16)).astype(jnp.float32)

@jax.custom_vjp
def low_back(v):
    return v

def low_keep(v):
    return (low(v), None)

def low_pass(kept, grad):
    return (grad,)

def back_keep(v):
    return (v, None)

def back_low(kept, grad):
    return (low(grad),)
low.defvjp(low_keep, low_pass)
low_back.defvjp(back_keep, back_low)
EPS = 1e-05
THETA = 10000.0
NEG = -1e+30
HIGHEST = lax.Precision.HIGHEST

def rms_norm(values, gain_row):
    return values * lax.rsqrt(lax.optimization_barrier(jnp.mean(values * values, axis=-1, keepdims=True)) + EPS) * gain_row

def rope_tables(position):
    halfway = HD // 2
    frequency = THETA ** (-(jnp.arange(halfway, dtype=jnp.float32) * 2.0 / HD))
    angles = position[:, None] * frequency[None, :]
    return (jnp.cos(angles), jnp.sin(angles))

def rotate(values, cosine, sine_part):
    halfway = values.shape[-1] // 2
    leading = values[..., :halfway]
    trailing = values[..., halfway:]
    return jnp.concatenate([leading * cosine - trailing * sine_part, trailing * cosine + leading * sine_part], axis=-1)

def segment_info(lengths_row, row_total):
    index_all = jnp.arange(row_total, dtype=jnp.int32)
    ends_at = jnp.cumsum(lengths_row)
    segment = lax.optimization_barrier(jnp.sum((index_all[:, None] >= ends_at[None, :]).astype(jnp.int32), axis=1))
    starts_at = ends_at - lengths_row
    numbers = jnp.arange(lengths_row.shape[0], dtype=jnp.int32)
    begins = lax.optimization_barrier(jnp.sum(jnp.where(segment[:, None] == numbers[None, :], starts_at[None, :], 0), axis=1))
    return (index_all, segment, (index_all - begins).astype(jnp.float32))

def layer_group(group_in, lengths_row, route_rows, gain_rows, router_f, qkv_f, out_f, in_f, exp_out_f):
    row_total = group_in.shape[0]
    index_all, segment, position = segment_info(lengths_row, row_total)
    cosine, sine_part = rope_tables(position)
    normed_first = low(rms_norm(group_in, gain_rows[0]))
    projected = low_back(jnp.einsum('td,hdc->htc', normed_first, qkv_f, precision=HIGHEST))
    queries = projected[:, :, :GRP * HD].reshape(KV, row_total, GRP, HD).transpose(0, 2, 1, 3)
    queries = low(rotate(queries, cosine, sine_part))
    keys_rot = low(rotate(projected[:, :, GRP * HD:(GRP + 1) * HD], cosine, sine_part))
    values_low = low(projected[:, :, (GRP + 1) * HD:])
    allowed = (segment[:, None] == segment[None, :]) & (index_all[None, :] <= index_all[:, None])
    scale_factor = HD ** (-0.5)

    def one_head(packed):
        query_head, key_head, value_head = packed
        scores = low_back(jnp.einsum('gqc,kc->gqk', query_head, key_head, precision=HIGHEST) * scale_factor)
        probability = jax.nn.softmax(jnp.where(allowed[None], scores, NEG), axis=-1)
        return low_back(low(jnp.einsum('gqk,kc->gqc', low(probability), value_head, precision=HIGHEST)))
    attended = lax.map(jax.checkpoint(one_head), (queries, keys_rot, values_low))
    mixed = low_back(jnp.einsum('hgtc,hgcd->td', attended, out_f.reshape(KV, GRP, HD, D), precision=HIGHEST))
    residual = group_in + mixed
    normed_second = low(rms_norm(residual, gain_rows[1]))
    logits = jnp.dot(normed_second, router_f, precision=HIGHEST)
    chosen = jnp.take_along_axis(logits, route_rows, axis=1)
    gates = jax.nn.softmax(chosen, axis=-1)
    expert_ids = jnp.arange(E, dtype=jnp.int32)
    route_hits = route_rows[:, :, None] == expert_ids[None, None, :]
    gate_dense = lax.optimization_barrier(jnp.sum(gates[:, :, None] * route_hits.astype(jnp.float32), axis=1))
    member = lax.optimization_barrier(jnp.sum(route_hits.astype(jnp.int32), axis=1))
    block_total = row_total // TOK_DEV

    def one_block(packed):
        block_rows, gate_rows, member_rows = packed
        places = jnp.cumsum(member_rows, axis=0) - 1
        slot_ids = jnp.arange(MOST, dtype=jnp.int32)
        selected = (member_rows.T[:, None, :] == 1) & (places.T[:, None, :] == slot_ids[None, :, None])
        row_ids = jnp.arange(TOK_DEV, dtype=jnp.int32)
        token_of = lax.optimization_barrier(jnp.sum(jnp.where(selected, row_ids[None, None, :], 0), axis=2)).astype(jnp.int32)
        filled = jnp.any(selected, axis=2).astype(jnp.float32)
        taken = low_back(block_rows[token_of] * filled[:, :, None])
        gate_up = low_back(jnp.einsum('esd,edf->esf', taken, in_f, precision=HIGHEST))
        hidden = low(jax.nn.silu(gate_up[..., :F]) * gate_up[..., F:])
        produced = low_back(jnp.einsum('esf,efd->esd', hidden, exp_out_f, precision=HIGHEST))
        slot_gate = gate_rows[token_of, expert_ids[:, None]] * filled
        scaled = low(slot_gate[..., None] * produced)
        return jnp.zeros((TOK_DEV, D), jnp.float32).at[token_of.reshape(-1)].add(scaled.reshape(-1, D))
    expert_mix = lax.map(jax.checkpoint(one_block), (normed_second.reshape(block_total, TOK_DEV, D), gate_dense.reshape(block_total, TOK_DEV, E), member.reshape(block_total, TOK_DEV, E)))
    expert_mix = low_back(expert_mix.reshape(row_total, D))
    return residual + expert_mix

def reference(tokens, cotangent, lengths, routes, norm_gains, router_weight, qkv_weight, out_weight, expert_in, expert_out):

    def forward(inputs, gain_rows, router_f, qkv_f, out_f, in_f, exp_out_f):

        def one_group(packed):
            group_in, lengths_row, route_rows = packed
            return layer_group(group_in, lengths_row, route_rows, gain_rows, router_f, qkv_f, out_f, in_f, exp_out_f)
        stacked = lax.map(jax.checkpoint(one_group), (inputs.reshape(N_DP, GROUP_TOK, D), lengths, routes.reshape(N_DP, GROUP_TOK, TOP)))
        return stacked.reshape(TOKENS, D)
    result, pullback = jax.vjp(forward, tokens.astype(jnp.float32), norm_gains.astype(jnp.float32), router_weight.astype(jnp.float32), qkv_weight.astype(jnp.float32), out_weight.astype(jnp.float32), expert_in.astype(jnp.float32), expert_out.astype(jnp.float32))
    gradients = pullback(cotangent.astype(jnp.float32))
    return (result.astype(jnp.bfloat16), gradients[0], gradients[1], gradients[2], gradients[3], gradients[4], gradients[5], gradients[6])
```

```python
import functools

import jax
import jax.numpy as jnp
from jax import lax
from jax.experimental import pallas as pl
from jax.experimental.pallas import tpu as pltpu
from jax.sharding import PartitionSpec as P

HD = 64
GRP = 3
F = 512
QF = F // 4
E = 40
BLK = 256
SLOT = 88
WIN_BLOCKS = 512 // BLK
EPS = 1e-05
THETA = 10000.0
NEG = -1e30
SCALE = HD ** (-0.5)
WCOLS = 2 * F + 2 * QF + F + QF
VMEM = 60 * 1024 * 1024
BF = jnp.bfloat16
F32 = jnp.float32


def dot_nn(a, b):
    return lax.dot_general(a, b, (((1,), (0,)), ((), ())), preferred_element_type=F32)


def dot_nt(a, b):
    return lax.dot_general(a, b, (((1,), (1,)), ((), ())), preferred_element_type=F32)


def dot_tn(a, b):
    return lax.dot_general(a, b, (((0,), (0,)), ((), ())), preferred_element_type=F32)


def params(**kw):
    return pltpu.CompilerParams(vmem_limit_bytes=VMEM, **kw)


def whole(shape):
    return pl.BlockSpec(shape, lambda *a: (0,) * len(shape), pipeline_mode=pl.Buffered(1))


class Links:
    def __init__(self, group):
        self.n_dp = lax.axis_size("dp")
        self.n_t = lax.axis_size("tensor")
        self.group = group
        self.fast = self.n_dp == 8 and self.n_t == 4 and group == 8
        self.dp = lax.axis_index("dp")
        self.t = lax.axis_index("tensor")
        if self.fast:
            devices = [(d, t) for d in range(8) for t in range(4)]
            number = lambda d, t: d * 4 + t
            ring = {0: 1, 1: 3, 3: 2, 2: 0}
            self.first = [(number(d, t), number(d, t ^ (2 if d & 1 else 1))) for d, t in devices]
            self.second = [(number(d, t), number(d, t ^ (1 if d & 1 else 2))) for d, t in devices]
            self.swap = [(number(d, t), number(d ^ 1, t)) for d, t in devices]
            self.along = [(number(d, t), number(ring[d >> 1] * 2 + (d & 1), t)) for d, t in devices]

    def send(self, value, perm):
        return lax.ppermute(value, ("dp", "tensor"), perm)

    def plane_order(self, core):
        one = jnp.where(core == 0, 1, 2)
        return [self.t, self.t ^ one, self.t ^ (3 - one), self.t ^ 3]

    def plane_places(self):
        if not self.fast:
            return jnp.arange(self.n_t, dtype=jnp.int32)
        one = jnp.where((self.dp & 1) == 0, 1, 2)
        diff = jnp.arange(4, dtype=jnp.int32) ^ self.t
        return jnp.where(diff == one, 1, jnp.where(diff == 3 - one, 2, diff)).astype(jnp.int32)

    def gather_plane(self, block):
        if not self.fast:
            return lax.all_gather(block, "tensor", axis=0)
        near = self.send(block, self.first)
        other = self.send(block, self.second)
        far = self.send(near, self.second)
        return jnp.stack([block, near, other, far])

    def scatter_plane(self, parts):
        if not self.fast:
            rows = parts.reshape((-1,) + parts.shape[2:])
            return lax.psum_scatter(rows, "tensor", scatter_dimension=0, tiled=True)
        a, b = self.scatter_plane_open(parts)
        return add(a, b)

    def scatter_plane_open(self, parts):
        got_far = self.send(parts[3], self.second)
        got = self.send(parts[2], self.second)
        got_near = self.send(add(parts[1], got_far), self.first)
        return add(parts[0], got), got_near

    def chunks(self):
        return self.group * self.n_t // 8

    def chunk_sources(self):
        if not self.fast:
            base = (self.dp // self.group) * self.group * self.n_t
            return [base + 8 * c + jnp.arange(8, dtype=jnp.int32) for c in range(self.chunks())]
        z, core = self.dp >> 1, self.dp & 1
        place = z ^ (z >> 1)
        out = []
        for c in range(4):
            back = (place + 4 - c) & 3
            source = back ^ (back >> 1)
            rows = [(source * 2 + core) * 4 + t for t in self.plane_order(core)]
            rows += [(source * 2 + 1 - core) * 4 + t for t in self.plane_order(1 - core)]
            out.append(jnp.stack(rows).astype(jnp.int32))
        return out

    def groups(self):
        n = self.n_dp // self.group
        return [list(range(g * self.group, (g + 1) * self.group)) for g in range(n)]

    def gather_all(self, block):
        if not self.fast:
            plane = lax.all_gather(block, "tensor", axis=0)
            rows = lax.all_gather(plane, "dp", axis=0, axis_index_groups=self.groups())
            rows = rows.reshape((-1,) + block.shape)
            return [(rows[8 * c : 8 * c + 4], rows[8 * c + 4 : 8 * c + 8]) for c in range(self.chunks())]
        out = []
        for c in range(4):
            mine = self.gather_plane(block)
            out.append((mine, self.send(mine, self.swap)))
            if c < 3:
                block = self.send(block, self.along)
        return out

    def scatter_chunk(self, mine, theirs):
        return self.scatter_plane(add(mine, self.send(theirs, self.swap)))

    def scatter_all(self, pairs):
        if not self.fast:
            rows = jnp.concatenate([half for pair in pairs for half in pair])
            rows = rows.reshape((self.group, -1) + rows.shape[2:])
            total = lax.psum_scatter(rows, "dp", scatter_dimension=0, axis_index_groups=self.groups())
            total = lax.psum_scatter(total, "tensor", scatter_dimension=0, tiled=True)
            return total, jnp.zeros_like(total)
        sums = [self.scatter_chunk(*pair) for pair in pairs]
        moving = self.send(sums[1], self.along)
        moving = self.send(add(moving, sums[2]), self.along)
        moving = self.send(add(moving, sums[3]), self.along)
        return sums[0], moving


def add(a, b):
    return (a.astype(F32) + b.astype(F32)).astype(a.dtype)


def pack_kernel(full_ref, gate_ref, up_ref, out_ref, quarter_ref, packed_ref):
    packed_ref[0, :, : 2 * F] = full_ref[0]
    packed_ref[0, :, 2 * F : 2 * F + QF] = gate_ref[0]
    packed_ref[0, :, 2 * F + QF : 2 * F + 2 * QF] = up_ref[0]
    packed_ref[0, :, 2 * F + 2 * QF : 3 * F + 2 * QF] = out_ref[0].astype(F32).T.astype(BF)
    packed_ref[0, :, 3 * F + 2 * QF :] = quarter_ref[0].astype(F32).T.astype(BF)


def pack_experts(expert_in, expert_out, group, n_dp):
    depth = expert_in.shape[1]
    of = lambda d: d % group
    return pl.pallas_call(
        pack_kernel,
        grid=(n_dp,),
        in_specs=[
            pl.BlockSpec((1, depth, 2 * F), lambda d: (of(d), 0, 0)),
            pl.BlockSpec((1, depth, QF), lambda d: (group + of(d) // 4, 0, of(d) % 4)),
            pl.BlockSpec((1, depth, QF), lambda d: (group + of(d) // 4, 0, 4 + of(d) % 4)),
            pl.BlockSpec((1, F, depth), lambda d: (of(d), 0, 0)),
            pl.BlockSpec((1, QF, depth), lambda d: (group + of(d) // 4, of(d) % 4, 0)),
        ],
        out_specs=pl.BlockSpec((1, depth, WCOLS), lambda d: (d, 0, 0)),
        out_shape=jax.ShapeDtypeStruct((n_dp, depth, WCOLS), BF),
        compiler_params=params(),
        name="pack_experts",
    )(expert_in, expert_in, expert_in, expert_out, expert_out)


def unpack_kernel(group, packed_ref, in_ref, out_ref):
    e = pl.program_id(0)

    @pl.when(e < group)
    def _():
        in_ref[0] = packed_ref[e, :, : 2 * F].astype(F32)
        out_ref[0] = packed_ref[e, :, 2 * F + 2 * QF : 3 * F + 2 * QF].astype(F32).T

    @pl.when(e >= group)
    def _():
        for q in range(4):
            s = (e - group) * 4 + q
            in_ref[0, :, q * QF : (q + 1) * QF] = packed_ref[s, :, 2 * F : 2 * F + QF].astype(F32)
            in_ref[0, :, F + q * QF : F + (q + 1) * QF] = packed_ref[
                s, :, 2 * F + QF : 2 * F + 2 * QF
            ].astype(F32)
            out_ref[0, q * QF : (q + 1) * QF, :] = packed_ref[s, :, 3 * F + 2 * QF :].astype(F32).T


def unpack_experts(packed, experts, group):
    depth = packed.shape[1]
    return pl.pallas_call(
        functools.partial(unpack_kernel, group),
        grid=(experts,),
        in_specs=[whole(packed.shape)],
        out_specs=(
            pl.BlockSpec((1, depth, 2 * F), lambda e: (e, 0, 0)),
            pl.BlockSpec((1, F, depth), lambda e: (e, 0, 0)),
        ),
        out_shape=(
            jax.ShapeDtypeStruct((experts, depth, 2 * F), F32),
            jax.ShapeDtypeStruct((experts, F, depth), F32),
        ),
        compiler_params=params(),
        name="unpack_experts",
    )(packed)


def expert_kernel(info_ref, xa_ref, xb_ref, ya_ref, yb_ref, routes_ref, router_ref, w_ref, *rest):
    ma_ref, mb_ref, da_ref, db_ref, taken_ref, dz_ref, dgu_ref, hid_ref = rest[-8:]
    step = pl.program_id(0)
    first, second = info_ref[0], info_ref[1]
    expert_id = lax.broadcasted_iota(jnp.int32, (E, BLK), 0)
    slot_id = lax.broadcasted_iota(jnp.int32, (SLOT, BLK), 0)
    upto = (
        lax.broadcasted_iota(jnp.int32, (BLK, BLK), 0) <= lax.broadcasted_iota(jnp.int32, (BLK, BLK), 1)
    ).astype(BF)
    row_id = lax.broadcasted_iota(jnp.int32, (8, BLK), 0)
    picks, slot_gates, taken, dz = [], ([], []), ([], []), ([], [])
    for b in range(4):
        x_ref, y_ref = (xa_ref, ya_ref) if b < 2 else (xb_ref, yb_ref)
        x, y = x_ref[b % 2], y_ref[b % 2]
        place = step * 2 + b % 2 + (0 if b < 2 else 4)
        routes = routes_ref[info_ref[2 + place]]
        logits = dot_nt(router_ref[...], x)[:E]
        member = expert_id == routes[0:1]
        for k in range(1, 8):
            member = member | (expert_id == routes[k : k + 1])
        masked = jnp.where(member, logits, NEG)
        shifted = jnp.exp(masked - jnp.max(masked, axis=0, keepdims=True))
        shifted = jnp.where(member, shifted, 0.0)
        gates = shifted / jnp.sum(shifted, axis=0, keepdims=True)
        member = member.astype(F32)
        rows = []
        for e in (first, second):
            here = expert_id == e
            rows.append(
                (
                    jnp.sum(jnp.where(here, gates, 0.0), axis=0, keepdims=True),
                    jnp.sum(jnp.where(here, member, 0.0), axis=0, keepdims=True),
                )
            )
        both = jnp.where(row_id == 0, rows[0][1], jnp.where(row_id == 1, rows[1][1], 0.0))
        counts = dot_nn(both.astype(BF), upto).astype(jnp.int32)
        pick = []
        for j in range(2):
            spot = jnp.where(rows[j][1] > 0.0, counts[j : j + 1] - 1, -1)
            hot = (slot_id == spot).astype(F32)
            slot_gates[j].append(jnp.sum(hot * rows[j][0], axis=1, keepdims=True))
            pick.append(hot)
        pick = jnp.concatenate(pick, axis=0).astype(BF)
        picks.append(pick)
        got = dot_nn(pick, x)
        taken[0].append(got[:SLOT])
        taken[1].append(got[SLOT:])
        got = dot_nn(pick, y)
        dz[0].append(got[:SLOT])
        dz[1].append(got[SLOT:])
    sends, backs = [], []
    for j in range(2):
        width = F if j == 0 else QF
        in_at = 0 if j == 0 else 2 * F
        out_at = 2 * F + 2 * QF + (0 if j == 0 else F)
        rows = jnp.concatenate(taken[j], axis=0).astype(BF)
        grads = jnp.concatenate(dz[j], axis=0).astype(BF)
        gate = jnp.concatenate(slot_gates[j], axis=0)
        taken_ref[0, j] = rows
        dz_ref[0, j] = grads
        w_in = w_ref[:, in_at : in_at + 2 * width]
        w_out = w_ref[:, out_at : out_at + width]
        gate_up = dot_nn(rows, w_in)
        gate_part, up_part = gate_up[:, :width], gate_up[:, width:]
        sig = 1.0 / (1.0 + jnp.exp(-gate_part))
        silu = gate_part * sig
        hidden = silu * up_part
        scaled = (gate * hidden).astype(BF)
        hid_at = 0 if j == 0 else F
        hid_ref[0, :, hid_at : hid_at + width] = scaled
        sends.append(dot_nt(scaled, w_out))
        raw = dot_nn(grads, w_out)
        dgate = jnp.sum(hidden.astype(BF).astype(F32) * raw, axis=1, keepdims=True)
        dhid = gate * raw
        dgu = jnp.concatenate(
            [dhid * up_part * (sig * (1.0 + gate_part * (1.0 - sig))), dhid * silu], axis=1
        ).astype(BF)
        dgu_ref[0, :, in_at : in_at + 2 * width] = dgu
        back = dot_nt(dgu, w_in)
        lane = lax.broadcasted_iota(jnp.int32, (1, 128), 1)
        e = first if j == 0 else second
        high = dgate.astype(BF).astype(F32)
        extra = jnp.where(lane == e, high, 0.0) + jnp.where(lane == e + 64, dgate - high, 0.0)
        backs.append(jnp.concatenate([back, extra], axis=1))
    for b in range(4):
        m_ref, d_ref = (ma_ref, da_ref) if b < 2 else (mb_ref, db_ref)
        at = slice(b * SLOT, (b + 1) * SLOT)
        for values, ref in ((sends, m_ref), (backs, d_ref)):
            stacked = jnp.concatenate([values[0][at], values[1][at]], axis=0).astype(BF)
            ref[b % 2] = dot_tn(picks[b], stacked).astype(BF)


def expert_chunk(chunk, chunks, info, rows, grads, routes, router_t, weights, stash):
    width = rows[0].shape[-1]
    steps = 2
    half = pl.BlockSpec((2, BLK, width), lambda s, i: (s, 0, 0))
    half_wide = pl.BlockSpec((2, BLK, width + 128), lambda s, i: (s, 0, 0))
    slots = 4 * SLOT
    total = chunks * steps
    shape = jax.ShapeDtypeStruct
    stash_shapes = [
        shape((total, 2, slots, width), BF),
        shape((total, 2, slots, width), BF),
        shape((total, slots, 2 * F + 2 * QF), BF),
        shape((total, slots, F + QF), BF),
    ]
    stash_specs = [
        pl.BlockSpec(
            (1,) + s.shape[1:], lambda i, _, n=len(s.shape): (i + chunk * steps,) + (0,) * (n - 1)
        )
        for s in stash_shapes
    ]
    given = [] if stash is None else list(stash)
    out = pl.pallas_call(
        expert_kernel,
        grid_spec=pltpu.PrefetchScalarGridSpec(
            num_scalar_prefetch=1,
            grid=(steps,),
            in_specs=[half] * 4
            + [whole(routes.shape), whole(router_t.shape), whole(weights.shape)]
            + [pl.BlockSpec(memory_space=pl.ANY)] * len(given),
            out_specs=[half, half, half_wide, half_wide] + stash_specs,
        ),
        out_shape=[shape((4, BLK, width), BF)] * 2 + [shape((4, BLK, width + 128), BF)] * 2 + stash_shapes,
        input_output_aliases={8 + k: 4 + k for k in range(len(given))},
        compiler_params=params(),
        cost_estimate=pl.CostEstimate(flops=12 * 10**9, bytes_accessed=40 * 10**6, transcendentals=10**6),
        name="experts",
    )(info, rows[0], rows[1], grads[0], grads[1], routes, router_t, weights, *given)
    return (out[0], out[1]), (out[2], out[3]), out[4:]


def wgrad_kernel(steps, taken_ref, dz_ref, dgu_ref, hid_ref, out_ref, acc_ref):
    k = pl.program_id(0)
    flat = lambda v: v.reshape((-1, v.shape[-1]))

    def put(at, width, value):
        @pl.when(k == 0)
        def _():
            acc_ref[:, at : at + width] = value

        @pl.when(k > 0)
        def _():
            acc_ref[:, at : at + width] += value

    put(0, 2 * F, dot_tn(flat(taken_ref[:, 0]), flat(dgu_ref[:, :, : 2 * F])))
    put(2 * F, 2 * QF, dot_tn(flat(taken_ref[:, 1]), flat(dgu_ref[:, :, 2 * F :])))
    put(2 * F + 2 * QF, F, dot_tn(flat(dz_ref[:, 0]), flat(hid_ref[:, :, :F])))
    put(3 * F + 2 * QF, QF, dot_tn(flat(dz_ref[:, 1]), flat(hid_ref[:, :, F:])))

    @pl.when(k == steps - 1)
    def _():
        out_ref[...] = acc_ref[...].astype(BF)


def expert_wgrad(stash):
    taken, dz, dgu, hid = stash
    at_once = 2
    steps = taken.shape[0] // at_once
    width = taken.shape[-1]
    spec = lambda a: pl.BlockSpec((at_once,) + a.shape[1:], lambda k: (k,) + (0,) * (len(a.shape) - 1))
    return pl.pallas_call(
        functools.partial(wgrad_kernel, steps),
        grid=(steps,),
        in_specs=[spec(a) for a in stash],
        out_specs=whole((width, WCOLS)),
        out_shape=jax.ShapeDtypeStruct((width, WCOLS), BF),
        scratch_shapes=[pltpu.VMEM((width, WCOLS), F32)],
        compiler_params=params(),
        cost_estimate=pl.CostEstimate(flops=17 * 10**9, bytes_accessed=50 * 10**6, transcendentals=0),
        name="expert_wgrad",
    )(*stash)


def swap_halves(values):
    width = values.shape[1]
    lane = lax.broadcasted_iota(jnp.int32, values.shape, 1)
    up = pltpu.roll(values, width - HD // 2, 1)
    down = pltpu.roll(values, HD // 2, 1)
    return jnp.where((lane & (HD - 1)) < HD // 2, up, down)


def spread(table, width):
    return jnp.concatenate([table] * (width // 128), axis=1)


def allowed_mask(starts, block, window):
    first = (block - window + 1) * BLK
    shape = (BLK, window * BLK)
    query = block * BLK + lax.broadcasted_iota(jnp.int32, shape, 0)
    key = first + lax.broadcasted_iota(jnp.int32, shape, 1)
    begin = jnp.zeros(shape, jnp.int32)
    for s in starts:
        begin = jnp.where(query >= s, s, begin)
    return (key >= begin) & (key <= query)


def over_windows(block, blocks, body):
    for w in range(1, min(WIN_BLOCKS + 1, blocks) + 1):
        last = w == WIN_BLOCKS + 1
        pl.when((block >= w - 1) if last else (block == w - 1))(functools.partial(body, w))


def heads_to_rows(values, first):
    return jnp.concatenate([values[:, (first + g) * HD : (first + g + 1) * HD] for g in range(GRP)], axis=0)


def rows_to_heads(values):
    return [values[g * BLK : (g + 1) * BLK] for g in range(GRP)]


def attend_kernel(heads, blocks, seqs, info_ref, n1_ref, w_ref, cos_ref, sin_ref, out_ref, qkv_ref, o_ref, lse_ref):
    i = pl.program_id(0)
    q_wide, kv_wide = heads * GRP * HD, heads * HD
    rot_wide, qkv_wide = q_wide + kv_wide, q_wide + 2 * kv_wide
    projected = dot_nn(n1_ref[0], w_ref[:, :qkv_wide])
    turning = projected[:, :rot_wide]
    turned = turning * spread(cos_ref[...], rot_wide) + swap_halves(turning) * spread(sin_ref[...], rot_wide)
    rows = pl.ds(pl.multiple_of(i * BLK, BLK), BLK)
    queries = (turned[:, :q_wide].astype(BF).astype(F32) * SCALE).astype(BF)
    qkv_ref[rows, :q_wide] = queries
    qkv_ref[rows, q_wide:rot_wide] = turned[:, q_wide:].astype(BF)
    qkv_ref[rows, rot_wide:] = projected[:, rot_wide:].astype(BF)
    starts = [info_ref[blocks + s] for s in range(seqs)]

    def attend(window):
        keep = allowed_mask(starts, i, window)
        keys = pl.ds(pl.multiple_of((i - window + 1) * BLK, BLK), window * BLK)
        lane = lax.broadcasted_iota(jnp.int32, (BLK, 128), 1)
        lse_all = jnp.zeros((BLK, 128), F32)
        attended = []
        for h in range(heads):
            k_rows = qkv_ref[keys, q_wide + h * HD : q_wide + (h + 1) * HD]
            v_rows = qkv_ref[keys, rot_wide + h * HD : rot_wide + (h + 1) * HD]
            scores = dot_nt(heads_to_rows(queries, h * GRP), k_rows)
            for g in range(GRP):
                part = jnp.where(keep, scores[g * BLK : (g + 1) * BLK], NEG)
                top = jnp.max(part, axis=1, keepdims=True)
                shifted = jnp.exp(part - top)
                total = jnp.sum(shifted, axis=1, keepdims=True)
                probability = (shifted * (1.0 / total)).astype(BF)
                attended.append(dot_nn(probability, v_rows).astype(BF))
                lse_all = jnp.where(lane == h * GRP + g, top + jnp.log(total), lse_all)
        lse_ref[...] = lse_all
        attended = jnp.concatenate(attended, axis=1)
        o_ref[...] = attended
        out_ref[0] = dot_nt(attended, w_ref[:, qkv_wide:]).astype(BF)

    over_windows(i, blocks, attend)


def attend_forward(heads, info, normed, weights, cosine, sine, seqs):
    blocks, _, width = normed.shape
    rows = blocks * BLK
    q_wide = heads * GRP * HD
    qkv_wide = q_wide + 2 * heads * HD
    shape = jax.ShapeDtypeStruct
    return pl.pallas_call(
        functools.partial(attend_kernel, heads, blocks, seqs),
        grid_spec=pltpu.PrefetchScalarGridSpec(
            num_scalar_prefetch=1,
            grid=(blocks,),
            in_specs=[
                pl.BlockSpec((1, BLK, width), lambda i, info: (info[i], 0, 0)),
                whole(weights.shape),
                pl.BlockSpec((BLK, 128), lambda i, info: (i, 0)),
                pl.BlockSpec((BLK, 128), lambda i, info: (i, 0)),
            ],
            out_specs=[
                pl.BlockSpec((1, BLK, width), lambda i, info: (info[i], 0, 0)),
                whole((rows, qkv_wide)),
                pl.BlockSpec((BLK, q_wide), lambda i, info: (i, 0)),
                pl.BlockSpec((BLK, 128), lambda i, info: (i, 0)),
            ],
        ),
        out_shape=[
            shape((blocks, BLK, width), BF),
            shape((rows, qkv_wide), BF),
            shape((rows, q_wide), BF),
            shape((rows, 128), F32),
        ],
        compiler_params=params(),
        cost_estimate=pl.CostEstimate(flops=5 * 10**9, bytes_accessed=12 * 10**6, transcendentals=4 * 10**6),
        name="attend",
    )(info, normed, weights, cosine, sine)


def attend_back_kernel(
    heads,
    blocks,
    seqs,
    info_ref,
    da_ref,
    n1_ref,
    w_ref,
    cos_ref,
    sin_ref,
    qkv_ref,
    o_ref,
    lse_ref,
    dn1_ref,
    dw_ref,
    gain_ref,
    acc_ref,
    dq_ref,
    dkv_ref,
):
    step = pl.program_id(0)
    q_wide, kv_wide = heads * GRP * HD, heads * HD
    rot_wide, qkv_wide = q_wide + kv_wide, q_wide + 2 * kv_wide
    starts = [info_ref[blocks + s] for s in range(seqs)]

    @pl.when(step == 0)
    def _():
        acc_ref[...] = jnp.zeros_like(acc_ref)
        dkv_ref[...] = jnp.zeros_like(dkv_ref)
        gain_ref[...] = jnp.zeros_like(gain_ref)

    @pl.when(step < blocks)
    def _():
        i = step
        da = da_ref[0]
        w_out = w_ref[:, qkv_wide:]
        grad = dot_nn(da, w_out).astype(BF)
        acc_ref[:, qkv_wide:] += dot_tn(da, o_ref[...])
        rows = pl.ds(pl.multiple_of(i * BLK, BLK), BLK)
        queries = qkv_ref[rows, :q_wide]
        lse = lse_ref[...]

        def back(window):
            keep = allowed_mask(starts, i, window)
            keys = pl.ds(pl.multiple_of((i - window + 1) * BLK, BLK), window * BLK)
            for h in range(heads):
                k_rows = qkv_ref[keys, q_wide + h * HD : q_wide + (h + 1) * HD]
                v_rows = qkv_ref[keys, rot_wide + h * HD : rot_wide + (h + 1) * HD]
                stacked_q = heads_to_rows(queries, h * GRP)
                stacked_g = heads_to_rows(grad, h * GRP)
                scores = dot_nt(stacked_q, k_rows)
                dprob = dot_nt(stacked_g, v_rows)
                probs, dscores = [], []
                for g in range(GRP):
                    at = slice(g * BLK, (g + 1) * BLK)
                    one = h * GRP + g
                    prob = jnp.where(keep, jnp.exp(scores[at] - lse[:, one : one + 1]), 0.0)
                    both = prob * dprob[at]
                    inner = jnp.sum(both, axis=1, keepdims=True)
                    dscores.append((both - prob * inner).astype(BF))
                    probs.append(prob.astype(BF))
                probs = jnp.concatenate(probs, axis=0)
                dscores = jnp.concatenate(dscores, axis=0)
                dq = dot_nn(dscores, k_rows) * SCALE
                dq_ref[rows, h * GRP * HD : (h + 1) * GRP * HD] = jnp.concatenate(rows_to_heads(dq), axis=1)
                dkv_ref[h, keys, :HD] += dot_tn(dscores, stacked_q)
                dkv_ref[h, keys, HD:] += dot_tn(probs, stacked_g)

        over_windows(i, blocks, back)

    @pl.when(step >= blocks)
    def _():
        j = step - blocks
        rows = pl.ds(pl.multiple_of(j * BLK, BLK), BLK)
        dk = [dkv_ref[h, rows, :HD] for h in range(heads)]
        dv = [dkv_ref[h, rows, HD:] for h in range(heads)]
        turned = jnp.concatenate([dq_ref[rows, :]] + dk, axis=1)
        turned = turned * spread(cos_ref[...], rot_wide) - swap_halves(turned) * spread(sin_ref[...], rot_wide)
        dqkv = jnp.concatenate([turned] + dv, axis=1).astype(BF)
        n1 = n1_ref[0]
        acc_ref[:, :qkv_wide] += dot_tn(n1, dqkv)
        dn1 = dot_nt(dqkv, w_ref[:, :qkv_wide])
        gain_ref[...] += jnp.sum(dn1 * n1.astype(F32), axis=0, keepdims=True)
        dn1_ref[0] = dn1.astype(BF)

    @pl.when(step == 2 * blocks - 1)
    def _():
        dw_ref[...] = acc_ref[...].astype(BF)


def attend_backward(heads, info, da, normed, weights, cosine, sine, qkv, attended, lse, seqs):
    blocks, _, width = normed.shape
    rows = blocks * BLK
    q_wide = heads * GRP * HD
    shape = jax.ShapeDtypeStruct
    early = lambda i: jnp.minimum(i, blocks - 1)
    late = lambda i: jnp.maximum(i - blocks, 0)
    return pl.pallas_call(
        functools.partial(attend_back_kernel, heads, blocks, seqs),
        grid_spec=pltpu.PrefetchScalarGridSpec(
            num_scalar_prefetch=1,
            grid=(2 * blocks,),
            in_specs=[
                pl.BlockSpec((1, BLK, width), lambda i, info: (info[early(i)], 0, 0)),
                pl.BlockSpec((1, BLK, width), lambda i, info: (info[late(i)], 0, 0)),
                whole(weights.shape),
                pl.BlockSpec((BLK, 128), lambda i, info: (late(i), 0)),
                pl.BlockSpec((BLK, 128), lambda i, info: (late(i), 0)),
                whole(qkv.shape),
                pl.BlockSpec((BLK, q_wide), lambda i, info: (early(i), 0)),
                pl.BlockSpec((BLK, 128), lambda i, info: (early(i), 0)),
            ],
            out_specs=[
                pl.BlockSpec((1, BLK, width), lambda i, info: (info[late(i)], 0, 0)),
                whole(weights.shape),
                whole((1, width)),
            ],
            scratch_shapes=[
                pltpu.VMEM(weights.shape, F32),
                pltpu.VMEM((rows, q_wide), F32),
                pltpu.VMEM((heads, rows, 2 * HD), F32),
            ],
        ),
        out_shape=[shape((blocks, BLK, width), BF), shape(weights.shape, BF), shape((1, width), F32)],
        compiler_params=params(),
        cost_estimate=pl.CostEstimate(flops=14 * 10**9, bytes_accessed=25 * 10**6, transcendentals=4 * 10**6),
        name="attend_back",
    )(info, da, normed, weights, cosine, sine, qkv, attended, lse)


def residual_kernel(
    one_ref, two_ref, n2_ref, h_ref, gain_ref, router_ref, routes_ref, cot_ref, dh_ref, da_ref, dgain_ref, drouter_ref
):
    width = n2_ref.shape[1]
    total = one_ref[...].astype(F32) + two_ref[...].astype(F32)
    dn2 = total[:, :width]
    dgate = total[:, width:]
    dgate = dgate + pltpu.roll(dgate, 64, 1)
    n2 = n2_ref[...]
    logits = dot_nt(n2, router_ref[...])
    lane = lax.broadcasted_iota(jnp.int32, logits.shape, 1)
    routes = routes_ref[...]
    member = lane == routes[:, 0:1]
    for k in range(1, 8):
        member = member | (lane == routes[:, k : k + 1])
    masked = jnp.where(member, logits, NEG)
    shifted = jnp.where(member, jnp.exp(masked - jnp.max(masked, axis=1, keepdims=True)), 0.0)
    gates = shifted / jnp.sum(shifted, axis=1, keepdims=True)
    dgate = jnp.where(member, dgate, 0.0)
    dlogit = gates * (dgate - jnp.sum(gates * dgate, axis=1, keepdims=True))
    high = dlogit.astype(BF)
    low = (dlogit - high.astype(F32)).astype(BF)
    dn2 = dn2 + dot_nn(high, router_ref[...]) + dot_nn(low, router_ref[...])
    drouter_ref[...] = (dot_tn(high, n2) + dot_tn(low, n2))[:E]
    h = h_ref[...]
    inverse = lax.rsqrt(jnp.mean(h * h, axis=1, keepdims=True) + EPS)
    unit = h * inverse
    dgain_ref[...] = jnp.sum(dn2 * unit, axis=0, keepdims=True)
    inner = dn2 * gain_ref[...]
    dh = cot_ref[...].astype(F32) + inverse * (inner - unit * jnp.mean(inner * unit, axis=1, keepdims=True))
    dh_ref[...] = dh
    da_ref[...] = dh.astype(BF)


def residual_gradient(one, two, n2, h, gain, router_pad, routes, cotangent):
    rows, width = n2.shape
    shape = jax.ShapeDtypeStruct
    return pl.pallas_call(
        residual_kernel,
        out_shape=[
            shape((rows, width), F32),
            shape((rows, width), BF),
            shape((1, width), F32),
            shape((E, width), F32),
        ],
        compiler_params=params(),
        cost_estimate=pl.CostEstimate(flops=10**9, bytes_accessed=8 * 10**6, transcendentals=10**5),
        name="residual_gradient",
    )(one, two, n2, h, gain, router_pad, routes, cotangent)


def rms_unit(values):
    return values * lax.rsqrt(jnp.mean(values * values, axis=-1, keepdims=True) + EPS)


def rope_tables(starts, rows):
    index = jnp.arange(rows, dtype=jnp.int32)
    begin = jnp.max(jnp.where(index[:, None] >= starts[None, :], starts[None, :], 0), axis=1)
    position = (index - begin).astype(F32)
    halfway = HD // 2
    frequency = THETA ** (-(jnp.arange(halfway, dtype=F32) * 2.0 / HD))
    angles = position[:, None] * frequency[None, :]
    cosine, sine = jnp.cos(angles), jnp.sin(angles)
    return (
        jnp.concatenate([cosine] * 4, axis=1),
        jnp.concatenate([-sine, sine, -sine, sine], axis=1),
    )


def shards(tokens, cotangent, lengths, routes, norm_gains, router_weight, qkv_weight, out_weight, expert_in, expert_out):
    own_rows, width = tokens.shape
    group_rows = routes.shape[0]
    heads = qkv_weight.shape[0]
    experts = expert_in.shape[0]
    group = experts * 4 // 5
    n_dp = lax.axis_size("dp")
    links = Links(group)
    rank = links.dp % group
    own_expert = links.t * experts + rank
    part_expert = links.t * experts + group + rank // 4
    seqs = lengths.shape[1]
    blocks = group_rows // own_rows
    inputs = tokens.astype(F32)

    grouped = jnp.transpose(qkv_weight, (1, 0, 2))
    depth = grouped.shape[0]
    attention_shard = jnp.concatenate(
        [
            grouped[:, :, : GRP * HD].reshape(depth, -1),
            grouped[:, :, GRP * HD : (GRP + 1) * HD].reshape(depth, -1),
            grouped[:, :, (GRP + 1) * HD :].reshape(depth, -1),
            jnp.transpose(out_weight, (2, 0, 1)).reshape(depth, -1),
        ],
        axis=1,
    )
    attention_weights = lax.all_gather(attention_shard, "dp", axis=0, tiled=True)
    routes_own = jnp.transpose(routes).reshape(8, blocks, own_rows)
    routes_all = lax.all_gather(jnp.transpose(routes_own, (1, 0, 2)), "dp", axis=0, tiled=True)
    starts = jnp.cumsum(lengths[0]) - lengths[0]
    cosine, sine = rope_tables(starts, group_rows)
    info = jnp.concatenate([links.plane_places(), starts.astype(jnp.int32)])

    normed_first = (rms_unit(inputs) * norm_gains[0]).astype(BF)
    normed_group = links.gather_plane(normed_first)
    packed = pack_experts(expert_in, expert_out, group, n_dp)
    weights = lax.all_to_all(packed, "dp", 0, 0).reshape(width, WCOLS)
    grads = links.gather_all(cotangent)

    mixed, qkv, attended, lse = attend_forward(heads, info, normed_group, attention_weights, cosine, sine, seqs)
    residual = inputs + links.scatter_plane(mixed).astype(F32)
    normed_second = (rms_unit(residual) * norm_gains[1]).astype(BF)

    rows = links.gather_all(normed_second)
    router_t = jnp.transpose(router_weight)
    router_pad = jnp.pad(router_t, ((0, 128 - E), (0, 0)))
    mine = jnp.stack([own_expert, part_expert]).astype(jnp.int32)
    stash = None
    outs, backs = [], []
    for c, sources in enumerate(links.chunk_sources()):
        chunk_info = jnp.concatenate([mine, sources])
        out, back, stash = expert_chunk(
            c, links.chunks(), chunk_info, rows[c], grads[c], routes_all, router_t, weights, stash
        )
        outs.append(out)
        backs.append(back)
    one, two = links.scatter_all(backs)
    weights_grad = expert_wgrad(stash)
    returned = lax.all_to_all(weights_grad.reshape(n_dp, depth, WCOLS), "dp", 0, 0)
    if n_dp != group:
        returned = jnp.sum(returned.reshape(-1, group, depth, WCOLS).astype(F32), axis=0).astype(BF)
    expert_in_grad, expert_out_grad = unpack_experts(returned, experts, group)

    routes_mine = lax.dynamic_slice_in_dim(routes, links.t * own_rows, own_rows, 0)
    residual_grad, branch_grad, second_gain, router_part = residual_gradient(
        one, two, normed_second, residual, norm_gains[1:2], router_pad, routes_mine, cotangent
    )
    branch_group = links.gather_plane(branch_grad)
    dn1, attention_grad, first_gain = attend_backward(
        heads, info, branch_group, normed_group, attention_weights, cosine, sine, qkv, attended, lse, seqs
    )
    first_grad = links.scatter_plane(dn1).astype(F32)
    attention_mine = lax.psum_scatter(attention_grad, "dp", scatter_dimension=0, tiled=True).astype(F32)

    mix_one, mix_two = links.scatter_all(outs)
    layer_output = (residual + mix_one.astype(F32) + mix_two.astype(F32)).astype(BF)

    unit = rms_unit(inputs)
    inner = first_grad * norm_gains[0]
    inverse = lax.rsqrt(jnp.mean(inputs * inputs, axis=-1, keepdims=True) + EPS)
    input_grad = residual_grad + inverse * (inner - unit * jnp.mean(inner * unit, axis=-1, keepdims=True))

    router_sum = lax.psum(router_part, ("dp", "tensor"))
    gains = lax.psum(jnp.concatenate([first_gain / norm_gains[0:1], second_gain]), ("dp", "tensor"))

    q_wide, kv_wide = heads * GRP * HD, heads * HD
    split = lambda at, size: attention_mine[:, at : at + size].reshape(depth, heads, -1)
    qkv_grad = jnp.transpose(
        jnp.concatenate(
            [split(0, q_wide), split(q_wide, kv_wide), split(q_wide + kv_wide, kv_wide)], axis=2
        ),
        (1, 0, 2),
    )
    out_weight_grad = jnp.transpose(split(q_wide + 2 * kv_wide, q_wide), (1, 2, 0))
    return (
        layer_output,
        input_grad,
        gains,
        jnp.transpose(router_sum),
        qkv_grad,
        out_weight_grad,
        expert_in_grad,
        expert_out_grad,
    )


def solution(mesh):
    rows = P(("dp", "tensor"), None)
    return jax.shard_map(
        shards,
        mesh=mesh,
        in_specs=(
            rows,
            rows,
            P("dp", None),
            P("dp", None),
            P(),
            P(),
            P("tensor", "dp", None),
            P("tensor", None, "dp"),
            P("tensor", "dp", None),
            P("tensor", None, "dp"),
        ),
        out_specs=(
            rows,
            rows,
            P(),
            P(),
            P("tensor", "dp", None),
            P("tensor", None, "dp"),
            P("tensor", "dp", None),
            P("tensor", None, "dp"),
        ),
        check_vma=False,
    )
```

```python
import functools

import jax
import jax.numpy as jnp
from jax import lax
from jax.experimental import pallas as pl
from jax.experimental.pallas import tpu as pltpu
from jax.sharding import PartitionSpec as P

HD = 64
GRP = 3
F = 512
QF = F // 4
E = 40
BLK = 256
SLOT = 88
WIN_BLOCKS = 512 // BLK
EPS = 1e-05
THETA = 10000.0
NEG = -1e30
SCALE = HD ** (-0.5)
VMEM = 60 * 1024 * 1024
BF = jnp.bfloat16
COST = pl.CostEstimate(flops=10**6, bytes_accessed=10**4, transcendentals=0)
F32 = jnp.float32


def dot_nn(a, b):
    return lax.dot_general(a, b, (((1,), (0,)), ((), ())), preferred_element_type=F32)


def dot_nt(a, b):
    return lax.dot_general(a, b, (((1,), (1,)), ((), ())), preferred_element_type=F32)


def dot_tn(a, b):
    return lax.dot_general(a, b, (((0,), (0,)), ((), ())), preferred_element_type=F32)


def params(**kw):
    return pltpu.CompilerParams(vmem_limit_bytes=VMEM, **kw)


def whole(shape):
    return pl.BlockSpec(shape, lambda *a: (0,) * len(shape), pipeline_mode=pl.Buffered(1))


class Links:
    def __init__(self, group):
        self.n_dp = lax.axis_size("dp")
        self.n_t = lax.axis_size("tensor")
        self.group = group
        self.fast = self.n_dp == 8 and self.n_t == 4 and group == 8
        self.dp = lax.axis_index("dp")
        self.t = lax.axis_index("tensor")
        if self.fast:
            devices = [(d, t) for d in range(8) for t in range(4)]
            number = lambda d, t: d * 4 + t
            ring = {0: 1, 1: 3, 3: 2, 2: 0}
            self.first = [(number(d, t), number(d, t ^ (2 if d & 1 else 1))) for d, t in devices]
            self.second = [(number(d, t), number(d, t ^ (1 if d & 1 else 2))) for d, t in devices]
            self.swap = [(number(d, t), number(d ^ 1, t)) for d, t in devices]
            self.along = [(number(d, t), number(ring[d >> 1] * 2 + (d & 1), t)) for d, t in devices]
            self.against = [(b, a) for a, b in self.along]
            self.across = [(number(d, t), number(d ^ 6, t)) for d, t in devices]
            self.level = [[(number(d, t), number(d ^ (2 * k), t)) for d, t in devices] for k in range(4)]

    def send(self, label, value, perm, *later):
        value = after(value, *later)
        with jax.named_scope(label):
            return lax.ppermute(value, ("dp", "tensor"), perm)

    def plane_order(self, core):
        one = jnp.where(core == 0, 1, 2)
        return [self.t, self.t ^ one, self.t ^ (3 - one), self.t ^ 3]

    def plane_places(self):
        if not self.fast:
            return jnp.arange(self.n_t, dtype=jnp.int32)
        one = jnp.where((self.dp & 1) == 0, 1, 2)
        diff = jnp.arange(4, dtype=jnp.int32) ^ self.t
        return jnp.where(diff == one, 1, jnp.where(diff == 3 - one, 2, diff)).astype(jnp.int32)

    def gather_plane(self, block, *later):
        if not self.fast:
            return lax.all_gather(block, "tensor", axis=0)
        near = self.send("plane_near", block, self.first, *later)
        pair = jnp.stack([block, near])
        return jnp.concatenate([pair, self.send("plane_far", pair, self.second)])

    def scatter_plane(self, parts, *later):
        if not self.fast:
            rows = parts.reshape((-1,) + parts.shape[2:])
            return [lax.psum_scatter(rows, "tensor", scatter_dimension=0, tiled=True)]
        got = self.send("parts_far", parts[2:], self.second, *later)
        return [parts[0], got[0], self.send("parts_near", add(parts[1], got[1]), self.first)]

    def chunks(self):
        return self.group * self.n_t // 8

    def chunk_sources(self):
        if not self.fast:
            base = (self.dp // self.group) * self.group * self.n_t
            own = [8 * c + jnp.arange(8, dtype=jnp.int32) for c in range(self.chunks())]
            return [base + o for o in own]
        z, core = self.dp >> 1, self.dp & 1
        place = z ^ (z >> 1)
        out = []
        for c in range(4):
            back = (place + 4 - c) & 3
            source = back ^ (back >> 1)
            mine, theirs = self.plane_order(core), self.plane_order(1 - core)
            routes = [(source ^ z) * 4 + t for t in mine] + [((source ^ z) + 4) * 4 + t for t in theirs]
            out.append(jnp.stack(routes).astype(jnp.int32))
        return out

    def groups(self):
        n = self.n_dp // self.group
        return [list(range(g * self.group, (g + 1) * self.group)) for g in range(n)]

    def gather_group(self, block):
        if self.n_dp == self.group:
            return lax.all_gather(block, ("dp", "tensor"), axis=0)
        plane = lax.all_gather(block, "tensor", axis=0)
        return lax.all_gather(plane, "dp", axis=0, axis_index_groups=self.groups()).reshape((-1,) + block.shape)

    def scatter_group(self, pairs):
        rows = jnp.concatenate([half for pair in pairs for half in pair])
        rows = rows.reshape((self.group, -1) + rows.shape[2:])
        total = lax.psum_scatter(rows, "dp", scatter_dimension=0, axis_index_groups=self.groups())
        return [lax.psum_scatter(total, "tensor", scatter_dimension=0, tiled=True)]

    def sum_all(self, value, *later):
        if not self.fast:
            return lax.psum(value, ("dp", "tensor"))
        for perm in (self.swap, self.first, self.second):
            value = value + self.send("small", value, perm)
        value = after(value, *later)
        for perm in self.level[1:3]:
            value = value + self.send("small", value, perm)
        return value


def after(value, *earlier):
    return lax.optimization_barrier((value,) + earlier)[0] if earlier else value


def total_of(parts):
    total = parts[0].astype(F32)
    for part in parts[1:]:
        total = total + part.astype(F32)
    return total


def add(a, b):
    return (a.astype(F32) + b.astype(F32)).astype(a.dtype)


def pack_attention_kernel(heads, qkv_ref, out_ref, packed_ref):
    q_wide, kv_wide = heads * GRP * HD, heads * HD
    for h in range(heads):
        one = qkv_ref[h]
        packed_ref[:, h * GRP * HD : (h + 1) * GRP * HD] = one[:, : GRP * HD]
        packed_ref[:, q_wide + h * HD : q_wide + (h + 1) * HD] = one[:, GRP * HD : (GRP + 1) * HD]
        at = q_wide + kv_wide + h * HD
        packed_ref[:, at : at + HD] = one[:, (GRP + 1) * HD :]
        at = q_wide + 2 * kv_wide + h * GRP * HD
        packed_ref[:, at : at + GRP * HD] = out_ref[h].astype(F32).T.astype(BF)


def pack_attention(qkv_weight, out_weight):
    heads, depth, _ = qkv_weight.shape
    return pl.pallas_call(
        functools.partial(pack_attention_kernel, heads),
        out_shape=jax.ShapeDtypeStruct((depth, heads * (2 * GRP + 2) * HD), BF),
        compiler_params=params(),
        name="pack_attention",
    )(qkv_weight, out_weight)


def attention_places(links):
    if not links.fast:
        return jnp.arange(links.n_dp, dtype=jnp.int32)
    z, core = links.dp >> 1, links.dp & 1
    near = [(z ^ k) * 2 for k in range(4)]
    return jnp.stack([n + core for n in near] + [n + 1 - core for n in near]).astype(jnp.int32)


def pack_kernel(gate_ref, up_ref, part_ref, down_ref, packed_ref):
    packed_ref[0, :, :QF] = gate_ref[0]
    packed_ref[0, :, QF : 2 * QF] = up_ref[0]
    packed_ref[0, :, 2 * QF : 3 * QF] = part_ref[0]
    packed_ref[0, :, 3 * QF :] = down_ref[0]


def pack_experts(expert_in, expert_out_t, group, n_dp):
    depth = expert_in.shape[1]
    of = lambda d: d % group
    return pl.pallas_call(
        pack_kernel,
        grid=(n_dp,),
        in_specs=[
            pl.BlockSpec((1, depth, QF), lambda d: (group + of(d) // 4, 0, of(d) % 4)),
            pl.BlockSpec((1, depth, QF), lambda d: (group + of(d) // 4, 0, 4 + of(d) % 4)),
            pl.BlockSpec((1, depth, QF), lambda d: (group + of(d) // 4, 0, of(d) % 4)),
            pl.BlockSpec((1, depth, F), lambda d: (of(d), 0, 0)),
        ],
        out_specs=pl.BlockSpec((1, depth, 3 * QF + F), lambda d: (d, 0, 0)),
        out_shape=jax.ShapeDtypeStruct((n_dp, depth, 3 * QF + F), BF),
        compiler_params=params(),
        name="pack_experts",
    )(expert_in, expert_in, expert_out_t, expert_out_t)


def unpack_kernel(group, full_ref, down_ref, part_ref, in_ref, out_ref):
    e = pl.program_id(0)

    @pl.when(e < group)
    def _():
        in_ref[0] = full_ref[0].astype(F32)
        out_ref[0] = down_ref[0].astype(F32)

    @pl.when(e >= group)
    def _():
        for q in range(4):
            part = part_ref[(e - group) * 4 + q].astype(F32)
            in_ref[0, :, q * QF : (q + 1) * QF] = part[:, :QF]
            in_ref[0, :, F + q * QF : F + (q + 1) * QF] = part[:, QF : 2 * QF]
            out_ref[0, :, q * QF : (q + 1) * QF] = part[:, 2 * QF :]


def unpack_experts(full, down, part, experts, group):
    depth = full.shape[1]
    first = lambda e: (jnp.minimum(e, group - 1), 0, 0)
    return pl.pallas_call(
        functools.partial(unpack_kernel, group),
        grid=(experts,),
        in_specs=[
            pl.BlockSpec((1, depth, 2 * F), first),
            pl.BlockSpec((1, depth, F), first),
            whole(part.shape),
        ],
        out_specs=(
            pl.BlockSpec((1, depth, 2 * F), lambda e: (e, 0, 0)),
            pl.BlockSpec((1, depth, F), lambda e: (e, 0, 0)),
        ),
        out_shape=(
            jax.ShapeDtypeStruct((experts, depth, 2 * F), F32),
            jax.ShapeDtypeStruct((experts, depth, F), F32),
        ),
        compiler_params=params(),
        name="unpack_experts",
    )(full, down, part)


def expert_kernel(
    info_ref, xa_ref, xb_ref, ya_ref, yb_ref, routes_ref, router_ref, full_ref, rest_ref,
    ma_ref, da_ref, theirs_ref, taken_ref, dz_ref, dgu_ref, hid_ref,
):
    step = pl.program_id(0)
    first, second = info_ref[0], info_ref[1]
    expert_id = lax.broadcasted_iota(jnp.int32, (E, BLK), 0)
    slot_id = lax.broadcasted_iota(jnp.int32, (SLOT, BLK), 0)
    upto = (
        lax.broadcasted_iota(jnp.int32, (BLK, BLK), 0) <= lax.broadcasted_iota(jnp.int32, (BLK, BLK), 1)
    ).astype(BF)
    row_id = lax.broadcasted_iota(jnp.int32, (8, BLK), 0)
    picks, slot_gates, taken, dz = [], ([], []), ([], []), ([], [])
    for b in range(4):
        x = (xa_ref if b < 2 else xb_ref)[b % 2].reshape(BLK, -1)
        y = (ya_ref if b < 2 else yb_ref)[b % 2].reshape(BLK, -1)
        routes = routes_ref[info_ref[2 + step * 2 + b % 2 + (0 if b < 2 else 4)]]
        logits = dot_nt(router_ref[...], x)
        member = expert_id == routes[0:1]
        for k in range(1, 8):
            member = member | (expert_id == routes[k : k + 1])
        masked = jnp.where(member, logits, NEG)
        shifted = jnp.exp(masked - jnp.max(masked, axis=0, keepdims=True))
        shifted = jnp.where(member, shifted, 0.0)
        gates = shifted / jnp.sum(shifted, axis=0, keepdims=True)
        member = member.astype(F32)
        rows = []
        for e in (first, second):
            here = expert_id == e
            rows.append(
                (
                    jnp.sum(jnp.where(here, gates, 0.0), axis=0, keepdims=True),
                    jnp.sum(jnp.where(here, member, 0.0), axis=0, keepdims=True),
                )
            )
        both = jnp.where(row_id == 0, rows[0][1], jnp.where(row_id == 1, rows[1][1], 0.0))
        counts = dot_nn(both.astype(BF), upto).astype(jnp.int32)
        pick = []
        for j in range(2):
            spot = jnp.where(rows[j][1] > 0.0, counts[j : j + 1] - 1, -1)
            hot = (slot_id == spot).astype(F32)
            slot_gates[j].append(jnp.sum(hot * rows[j][0], axis=1, keepdims=True))
            pick.append(hot)
        pick = jnp.concatenate(pick, axis=0).astype(BF)
        picks.append(pick)
        got = dot_nn(pick, x)
        taken[0].append(got[:SLOT])
        taken[1].append(got[SLOT:])
        got = dot_nn(pick, y)
        dz[0].append(got[:SLOT])
        dz[1].append(got[SLOT:])
    sends, backs = [], []
    for j in range(2):
        width = F if j == 0 else QF
        in_at = 0 if j == 0 else 2 * F
        rows = jnp.concatenate(taken[j], axis=0).astype(BF)
        grads = jnp.concatenate(dz[j], axis=0).astype(BF)
        gate = jnp.concatenate(slot_gates[j], axis=0)
        taken_ref[0, j] = rows
        dz_ref[0, j] = grads
        w_in = full_ref[...] if j == 0 else rest_ref[:, : 2 * QF]
        w_out = rest_ref[:, 3 * QF :] if j == 0 else rest_ref[:, 2 * QF : 3 * QF]
        gate_up = dot_nn(rows, w_in)
        gate_part, up_part = gate_up[:, :width], gate_up[:, width:]
        sig = 1.0 / (1.0 + jnp.exp(-gate_part))
        silu = gate_part * sig
        hidden = silu * up_part
        scaled = (gate * hidden).astype(BF)
        hid_at = 0 if j == 0 else F
        hid_ref[0, :, hid_at : hid_at + width] = scaled
        sends.append(dot_nt(scaled, w_out))
        raw = dot_nn(grads, w_out)
        dgate = jnp.sum(hidden.astype(BF).astype(F32) * raw, axis=1, keepdims=True)
        dhid = gate * raw
        dgu = jnp.concatenate(
            [dhid * up_part * (sig * (1.0 + gate_part * (1.0 - sig))), dhid * silu], axis=1
        ).astype(BF)
        dgu_ref[0, :, in_at : in_at + 2 * width] = dgu
        back = dot_nt(dgu, w_in)
        lane = lax.broadcasted_iota(jnp.int32, (1, 128), 1)
        e = first if j == 0 else second
        high = dgate.astype(BF).astype(F32)
        extra = jnp.where(lane == e, high, 0.0) + jnp.where(lane == e + 64, dgate - high, 0.0)
        backs.append(jnp.concatenate([back, extra], axis=1))
    for b in range(4):
        at = slice(b * SLOT, (b + 1) * SLOT)
        for kind, values in enumerate((backs, sends)):
            stacked = jnp.concatenate([values[0][at], values[1][at]], axis=0).astype(BF)
            summed = dot_tn(picks[b], stacked).astype(BF)
            if b < 2:
                (da_ref, ma_ref)[kind][b] = summed
            else:
                theirs_ref[kind, b - 2, :, : summed.shape[1]] = summed


def stepped(shape):
    return pl.BlockSpec((1,) + shape[1:], lambda s, *_: (s,) + (0,) * (len(shape) - 1))


def expert_chunk(info, rows, routes, router_t, weights):
    width = rows[0][0].shape[-1]
    shape = jax.ShapeDtypeStruct
    half = pl.BlockSpec((2, BLK, width), lambda s, i: (s, 0, 0))

    def given(array, column):
        if column is None:
            return half
        return pl.BlockSpec((2, 1, BLK, width), lambda s, i: (s, column, 0, 0))

    slots = 4 * SLOT
    kept = [
        shape((2, 2, slots, width), BF),
        shape((2, 2, slots, width), BF),
        shape((2, slots, 2 * F + 2 * QF), BF),
        shape((2, slots, F + QF), BF),
    ]
    return pl.pallas_call(
        expert_kernel,
        grid_spec=pltpu.PrefetchScalarGridSpec(
            num_scalar_prefetch=1,
            grid=(2,),
            in_specs=[given(*r) for r in rows] + [whole(a.shape) for a in (routes, router_t, *weights)],
            out_specs=[
                half,
                pl.BlockSpec((2, BLK, width + 128), lambda s, i: (s, 0, 0)),
                pl.BlockSpec((2, 2, BLK, width + 128), lambda s, i: (0, s, 0, 0)),
            ]
            + [stepped(s.shape) for s in kept],
        ),
        out_shape=[
            shape((4, BLK, width), BF),
            shape((4, BLK, width + 128), BF),
            shape((2, 4, BLK, width + 128), BF),
        ]
        + kept,
        compiler_params=params(),
        cost_estimate=pl.CostEstimate(flops=30 * 10**9, bytes_accessed=45 * 10**6, transcendentals=10**6),
        name="experts",
    )(info, *[r[0] for r in rows], routes, router_t, *weights)


def wgrad_kernel(chunks, pairs, *refs):
    out_ref = refs[-1]
    flat = lambda v: v.reshape((-1, v.shape[-1]))
    at = 0
    for p in range(pairs):
        left, right = refs[2 * p * chunks : (2 * p + 1) * chunks], refs[(2 * p + 1) * chunks : (2 * p + 2) * chunks]
        total = dot_tn(flat(left[0][...]), flat(right[0][...]))
        for l, r in zip(left[1:], right[1:]):
            total = total + dot_tn(flat(l[...]), flat(r[...]))
        out_ref[:, at : at + total.shape[1]] = total.astype(BF)
        at += total.shape[1]


def expert_wgrad(pairs, name):
    width = pairs[0][0][0].shape[-1]
    chunks = len(pairs[0][0])
    tile = 256
    specs, operands, columns = [], [], 0
    for left, j, right, at, size in pairs:
        rows = left[0].shape[2]
        specs += [pl.BlockSpec((2, 1, rows, tile), lambda k, j=j: (0, j, 0, k))] * chunks
        specs += [
            pl.BlockSpec((2, rows, size), lambda k, b=at // size: (0, 0, b), pipeline_mode=pl.Buffered(1))
        ] * chunks
        operands += list(left) + list(right)
        columns += size
    return pl.pallas_call(
        functools.partial(wgrad_kernel, chunks, len(pairs)),
        grid=(width // tile,),
        in_specs=specs,
        out_specs=pl.BlockSpec((tile, columns), lambda k: (k, 0)),
        out_shape=jax.ShapeDtypeStruct((width, columns), BF),
        compiler_params=params(),
        cost_estimate=COST,
        name=name,
    )(*operands)


def swap_halves(values):
    width = values.shape[1]
    lane = lax.broadcasted_iota(jnp.int32, values.shape, 1)
    up = pltpu.roll(values, width - HD // 2, 1)
    down = pltpu.roll(values, HD // 2, 1)
    return jnp.where((lane & (HD - 1)) < HD // 2, up, down)


def spread(table, width):
    return jnp.concatenate([table] * (width // 128), axis=1)


def allowed_mask(starts, block, window):
    first = (block - window + 1) * BLK
    shape = (BLK, window * BLK)
    query = block * BLK + lax.broadcasted_iota(jnp.int32, shape, 0)
    key = first + lax.broadcasted_iota(jnp.int32, shape, 1)
    begin = jnp.zeros(shape, jnp.int32)
    for s in starts:
        begin = jnp.where(query >= s, s, begin)
    return (key >= begin) & (key <= query)


def over_windows(block, blocks, body):
    for w in range(1, min(WIN_BLOCKS + 1, blocks) + 1):
        last = w == WIN_BLOCKS + 1
        pl.when((block >= w - 1) if last else (block == w - 1))(functools.partial(body, w))


def heads_to_rows(values, first):
    return jnp.concatenate([values[:, (first + g) * HD : (first + g + 1) * HD] for g in range(GRP)], axis=0)


def rows_to_heads(values):
    return [values[g * BLK : (g + 1) * BLK] for g in range(GRP)]


def attend_kernel(heads, blocks, seqs, pieces, info_ref, n1_ref, cos_ref, sin_ref, *refs):
    out_ref, qkv_ref, o_ref, lse_ref, w_ref = refs[pieces:]
    i = pl.program_id(0)

    @pl.when(i == 0)
    def _():
        each = [ref.at[p] for ref in refs[:pieces] for p in range(ref.shape[0])]
        depth = w_ref.shape[0] // len(each)
        for k, piece in enumerate(each):
            at = pl.multiple_of(info_ref[blocks + seqs + k] * depth, depth)
            w_ref[pl.ds(at, depth), :] = piece[:depth]

    q_wide, kv_wide = heads * GRP * HD, heads * HD
    rot_wide, qkv_wide = q_wide + kv_wide, q_wide + 2 * kv_wide
    projected = dot_nn(n1_ref[0], w_ref[:, :qkv_wide])
    turning = projected[:, :rot_wide]
    turned = turning * spread(cos_ref[...], rot_wide) + swap_halves(turning) * spread(sin_ref[...], rot_wide)
    rows = pl.ds(pl.multiple_of(i * BLK, BLK), BLK)
    queries = (turned[:, :q_wide].astype(BF).astype(F32) * SCALE).astype(BF)
    qkv_ref[rows, :q_wide] = queries
    qkv_ref[rows, q_wide:rot_wide] = turned[:, q_wide:].astype(BF)
    qkv_ref[rows, rot_wide:] = projected[:, rot_wide:].astype(BF)
    starts = [info_ref[blocks + s] for s in range(seqs)]

    def attend(window):
        keep = allowed_mask(starts, i, window)
        keys = pl.ds(pl.multiple_of((i - window + 1) * BLK, BLK), window * BLK)
        lane = lax.broadcasted_iota(jnp.int32, (BLK, 128), 1)
        lse_all = jnp.zeros((BLK, 128), F32)
        attended = []
        for h in range(heads):
            k_rows = qkv_ref[keys, q_wide + h * HD : q_wide + (h + 1) * HD]
            v_rows = qkv_ref[keys, rot_wide + h * HD : rot_wide + (h + 1) * HD]
            scores = dot_nt(heads_to_rows(queries, h * GRP), k_rows)
            for g in range(GRP):
                part = jnp.where(keep, scores[g * BLK : (g + 1) * BLK], NEG)
                top = jnp.max(part, axis=1, keepdims=True)
                shifted = jnp.exp(part - top)
                total = jnp.sum(shifted, axis=1, keepdims=True)
                probability = (shifted * (1.0 / total)).astype(BF)
                attended.append(dot_nn(probability, v_rows).astype(BF))
                lse_all = jnp.where(lane == h * GRP + g, top + jnp.log(total), lse_all)
        lse_ref[...] = lse_all
        attended = jnp.concatenate(attended, axis=1)
        o_ref[...] = attended
        out_ref[0] = dot_nt(attended, w_ref[:, qkv_wide:]).astype(BF)

    over_windows(i, blocks, attend)


def attend_forward(heads, info, normed, pieces, cosine, sine, seqs):
    blocks, _, width = normed.shape
    rows = blocks * BLK
    q_wide = heads * GRP * HD
    qkv_wide = q_wide + 2 * heads * HD
    shape = jax.ShapeDtypeStruct
    weights = (width, pieces[0].shape[-1])
    return pl.pallas_call(
        functools.partial(attend_kernel, heads, blocks, seqs, len(pieces)),
        grid_spec=pltpu.PrefetchScalarGridSpec(
            num_scalar_prefetch=1,
            grid=(blocks,),
            in_specs=[
                pl.BlockSpec((1, BLK, width), lambda i, info: (info[i], 0, 0)),
                pl.BlockSpec((BLK, 128), lambda i, info: (i, 0)),
                pl.BlockSpec((BLK, 128), lambda i, info: (i, 0)),
            ]
            + [whole(p.shape) for p in pieces],
            out_specs=[
                pl.BlockSpec((1, BLK, width), lambda i, info: (info[i], 0, 0)),
                whole((rows, qkv_wide)),
                pl.BlockSpec((BLK, q_wide), lambda i, info: (i, 0)),
                pl.BlockSpec((BLK, 128), lambda i, info: (i, 0)),
                whole(weights),
            ],
        ),
        out_shape=[
            shape((blocks, BLK, width), BF),
            shape((rows, qkv_wide), BF),
            shape((rows, q_wide), BF),
            shape((rows, 128), F32),
            shape(weights, BF),
        ],
        compiler_params=params(),
        cost_estimate=COST,
        name="attend",
    )(info, normed, cosine, sine, *pieces)


def attend_back_kernel(
    heads,
    blocks,
    seqs,
    info_ref,
    da_ref,
    n1_ref,
    w_ref,
    cos_ref,
    sin_ref,
    qkv_ref,
    o_ref,
    lse_ref,
    dn1_ref,
    dw_ref,
    gain_ref,
    acc_ref,
    dq_ref,
    dkv_ref,
):
    step = pl.program_id(0)
    q_wide, kv_wide = heads * GRP * HD, heads * HD
    rot_wide, qkv_wide = q_wide + kv_wide, q_wide + 2 * kv_wide
    starts = [info_ref[blocks + s] for s in range(seqs)]

    @pl.when(step == 0)
    def _():
        acc_ref[...] = jnp.zeros_like(acc_ref)
        dkv_ref[...] = jnp.zeros_like(dkv_ref)
        gain_ref[...] = jnp.zeros_like(gain_ref)

    @pl.when(step < blocks)
    def _():
        i = step
        da = da_ref[0]
        w_out = w_ref[:, qkv_wide:]
        grad = dot_nn(da, w_out).astype(BF)
        acc_ref[:, qkv_wide:] += dot_tn(da, o_ref[...])
        rows = pl.ds(pl.multiple_of(i * BLK, BLK), BLK)
        queries = qkv_ref[rows, :q_wide]
        lse = lse_ref[...]

        def back(window):
            keep = allowed_mask(starts, i, window)
            keys = pl.ds(pl.multiple_of((i - window + 1) * BLK, BLK), window * BLK)
            for h in range(heads):
                k_rows = qkv_ref[keys, q_wide + h * HD : q_wide + (h + 1) * HD]
                v_rows = qkv_ref[keys, rot_wide + h * HD : rot_wide + (h + 1) * HD]
                stacked_q = heads_to_rows(queries, h * GRP)
                stacked_g = heads_to_rows(grad, h * GRP)
                scores = dot_nt(stacked_q, k_rows)
                dprob = dot_nt(stacked_g, v_rows)
                probs, dscores = [], []
                for g in range(GRP):
                    at = slice(g * BLK, (g + 1) * BLK)
                    one = h * GRP + g
                    prob = jnp.where(keep, jnp.exp(scores[at] - lse[:, one : one + 1]), 0.0)
                    both = prob * dprob[at]
                    inner = jnp.sum(both, axis=1, keepdims=True)
                    dscores.append((both - prob * inner).astype(BF))
                    probs.append(prob.astype(BF))
                probs = jnp.concatenate(probs, axis=0)
                dscores = jnp.concatenate(dscores, axis=0)
                dq = dot_nn(dscores, k_rows) * SCALE
                dq_ref[rows, h * GRP * HD : (h + 1) * GRP * HD] = jnp.concatenate(rows_to_heads(dq), axis=1)
                dkv_ref[h, keys, :HD] += dot_tn(dscores, stacked_q)
                dkv_ref[h, keys, HD:] += dot_tn(probs, stacked_g)

        over_windows(i, blocks, back)

    @pl.when(step >= blocks)
    def _():
        j = step - blocks
        rows = pl.ds(pl.multiple_of(j * BLK, BLK), BLK)
        dk = [dkv_ref[h, rows, :HD] for h in range(heads)]
        dv = [dkv_ref[h, rows, HD:] for h in range(heads)]
        turned = jnp.concatenate([dq_ref[rows, :]] + dk, axis=1)
        turned = turned * spread(cos_ref[...], rot_wide) - swap_halves(turned) * spread(sin_ref[...], rot_wide)
        dqkv = jnp.concatenate([turned] + dv, axis=1).astype(BF)
        n1 = n1_ref[0]
        acc_ref[:, :qkv_wide] += dot_tn(n1, dqkv)
        dn1 = dot_nt(dqkv, w_ref[:, :qkv_wide])
        gain_ref[...] += jnp.sum(dn1 * n1.astype(F32), axis=0, keepdims=True)
        dn1_ref[0] = dn1.astype(BF)

    @pl.when(step == 2 * blocks - 1)
    def _():
        dw_ref[...] = acc_ref[...].astype(BF)


def attend_backward(heads, info, da, normed, weights, cosine, sine, qkv, attended, lse, seqs):
    blocks, _, width = normed.shape
    rows = blocks * BLK
    q_wide = heads * GRP * HD
    shape = jax.ShapeDtypeStruct
    early = lambda i: jnp.minimum(i, blocks - 1)
    late = lambda i: jnp.maximum(i - blocks, 0)
    return pl.pallas_call(
        functools.partial(attend_back_kernel, heads, blocks, seqs),
        grid_spec=pltpu.PrefetchScalarGridSpec(
            num_scalar_prefetch=1,
            grid=(2 * blocks,),
            in_specs=[
                pl.BlockSpec((1, BLK, width), lambda i, info: (info[early(i)], 0, 0)),
                pl.BlockSpec((1, BLK, width), lambda i, info: (info[late(i)], 0, 0)),
                whole(weights.shape),
                pl.BlockSpec((BLK, 128), lambda i, info: (late(i), 0)),
                pl.BlockSpec((BLK, 128), lambda i, info: (late(i), 0)),
                whole(qkv.shape),
                pl.BlockSpec((BLK, q_wide), lambda i, info: (early(i), 0)),
                pl.BlockSpec((BLK, 128), lambda i, info: (early(i), 0)),
            ],
            out_specs=[
                pl.BlockSpec((1, BLK, width), lambda i, info: (info[late(i)], 0, 0)),
                whole(weights.shape),
                whole((1, width)),
            ],
            scratch_shapes=[
                pltpu.VMEM(weights.shape, F32),
                pltpu.VMEM((rows, q_wide), F32),
                pltpu.VMEM((heads, rows, 2 * HD), F32),
            ],
        ),
        out_shape=[shape((blocks, BLK, width), BF), shape(weights.shape, BF), shape((1, width), F32)],
        compiler_params=params(),
        cost_estimate=COST,
        name="attend_back",
    )(info, da, normed, weights, cosine, sine, qkv, attended, lse)


def residual_kernel(parts, *refs):
    part_refs = refs[:parts]
    n2_ref, h_ref, gain_ref, router_ref, routes_ref, cot_ref, dh_ref, da_ref, dgain_ref, drouter_ref = refs[parts:]
    width = n2_ref.shape[1]
    total = total_of([r[...] for r in part_refs])
    dn2 = total[:, :width]
    dgate = total[:, width:]
    dgate = dgate + pltpu.roll(dgate, 64, 1)
    n2 = n2_ref[...]
    logits = dot_nt(n2, router_ref[...])
    lane = lax.broadcasted_iota(jnp.int32, logits.shape, 1)
    routes = routes_ref[...]
    member = lane == routes[:, 0:1]
    for k in range(1, 8):
        member = member | (lane == routes[:, k : k + 1])
    masked = jnp.where(member, logits, NEG)
    shifted = jnp.where(member, jnp.exp(masked - jnp.max(masked, axis=1, keepdims=True)), 0.0)
    gates = shifted / jnp.sum(shifted, axis=1, keepdims=True)
    dgate = jnp.where(member, dgate, 0.0)
    dlogit = gates * (dgate - jnp.sum(gates * dgate, axis=1, keepdims=True))
    high = dlogit.astype(BF)
    low = (dlogit - high.astype(F32)).astype(BF)
    dn2 = dn2 + dot_nn(high, router_ref[...]) + dot_nn(low, router_ref[...])
    drouter_ref[...] = (dot_tn(high, n2) + dot_tn(low, n2))[:E]
    h = h_ref[...]
    inverse = lax.rsqrt(jnp.mean(h * h, axis=1, keepdims=True) + EPS)
    unit = h * inverse
    dgain_ref[...] = jnp.sum(dn2 * unit, axis=0, keepdims=True)
    inner = dn2 * gain_ref[...]
    dh = cot_ref[...].astype(F32) + inverse * (inner - unit * jnp.mean(inner * unit, axis=1, keepdims=True))
    dh_ref[...] = dh
    da_ref[...] = dh.astype(BF)


def residual_gradient(parts, n2, h, gain, router_pad, routes, cotangent):
    rows, width = n2.shape
    shape = jax.ShapeDtypeStruct
    return pl.pallas_call(
        functools.partial(residual_kernel, len(parts)),
        out_shape=[
            shape((rows, width), F32),
            shape((rows, width), BF),
            shape((1, width), F32),
            shape((E, width), F32),
        ],
        compiler_params=params(),
        cost_estimate=COST,
        name="residual_gradient",
    )(*parts, n2, h, gain, router_pad, routes, cotangent)


def rms_unit(values):
    return values * lax.rsqrt(jnp.mean(values * values, axis=-1, keepdims=True) + EPS)


def rope_tables(starts, rows):
    index = jnp.arange(rows, dtype=jnp.int32)
    begin = jnp.max(jnp.where(index[:, None] >= starts[None, :], starts[None, :], 0), axis=1)
    position = (index - begin).astype(F32)
    halfway = HD // 2
    frequency = THETA ** (-(jnp.arange(halfway, dtype=F32) * 2.0 / HD))
    angles = position[:, None] * frequency[None, :]
    cosine, sine = jnp.cos(angles), jnp.sin(angles)
    return (
        jnp.concatenate([cosine] * 4, axis=1),
        jnp.concatenate([-sine, sine, -sine, sine], axis=1),
    )


def shards(tokens, cotangent, lengths, routes, norm_gains, router_weight, qkv_weight, out_weight, expert_in, expert_out):
    own_rows, width = tokens.shape
    group_rows = routes.shape[0]
    heads = qkv_weight.shape[0]
    experts, depth, _ = expert_in.shape
    group = experts * 4 // 5
    n_dp = lax.axis_size("dp")
    links = Links(group)
    fast = links.fast
    send, first, second = links.send, (links.first if fast else None), (links.second if fast else None)
    rank = links.dp % group
    own_expert = links.t * experts + rank
    part_expert = links.t * experts + group + rank // 4
    seqs = lengths.shape[1]
    blocks = group_rows // own_rows
    inputs = tokens.astype(F32)
    expert_out_t = jnp.swapaxes(expert_out, 1, 2)
    starts = jnp.cumsum(lengths[0]) - lengths[0]
    cosine, sine = rope_tables(starts, group_rows)
    info = jnp.concatenate([links.plane_places(), starts.astype(jnp.int32), attention_places(links)])
    router_t = jnp.transpose(router_weight)
    router_pad = jnp.pad(router_t, ((0, 128 - E), (0, 0)))
    mine = jnp.stack([own_expert, part_expert]).astype(jnp.int32)
    sources = links.chunk_sources()
    chunks = links.chunks()
    to_all = lambda a: lax.all_to_all(a, "dp", 0, 0)

    shard = pack_attention(qkv_weight, out_weight)
    normed_first = (rms_unit(inputs) * norm_gains[0]).astype(BF)
    packed = pack_experts(expert_in, expert_out_t, group, n_dp)
    own_in = expert_in[:group] if n_dp == group else jnp.concatenate([expert_in[:group]] * (n_dp // group))
    routes_t = jnp.transpose(routes)
    by_block = lambda r: jnp.transpose(r.reshape(-1, 8, blocks, own_rows), (0, 2, 1, 3)).reshape(-1, 8, own_rows)
    if fast:
        y, swap = cotangent, links.swap
        routes_rows = jnp.pad(routes_t.astype(BF), ((0, 8), (0, 0)))
        shard = jnp.concatenate([shard, routes_rows])
        pieces = [send("pieces", shard, links.level[k]) for k in range(1, 4)]
        near = send("near", normed_first, first, shard)
        pair = jnp.stack([normed_first, near])
        far = send("far", pair, second)

        pieces_mine = jnp.stack([shard] + pieces)
        pieces_theirs = send("pieces_theirs", pieces_mine, swap)
        y_near0 = send("y_near0", y, first, far)
        rest = to_all(after(packed, pieces_mine))
        normed_group = jnp.concatenate([pair, far])
        y_pair0 = jnp.stack([y, y_near0])
        y_far0 = send("y_far0", y_pair0, second)
        attend_pieces = [pieces_mine, pieces_theirs]
        routes_all = jnp.concatenate([pieces_mine[:, depth : depth + 8], pieces_theirs[:, depth : depth + 8]])
        routes_all = by_block(routes_all).astype(jnp.int32)
        before = (rest, y_far0)
    else:
        normed_group = links.gather_plane(normed_first)
        attend_pieces = [lax.all_gather(shard, "dp", axis=0)]
        rest = to_all(packed)
        routes_all = by_block(lax.all_gather(routes_t, "dp", axis=0))
        before = (packed,)
    mixed, qkv, attended, lse, attention_weights = attend_forward(
        heads, after(info, *before), normed_group, attend_pieces, cosine, sine, seqs
    )
    if fast:
        full = to_all(after(own_in, rest))
        h_far = send("h_far", mixed[2:], second)
        h_near = send("h_near", add(mixed[1], h_far[1]), first)
        y_mine0 = jnp.concatenate([y_pair0, after(y_far0, mixed)])
        y_theirs0 = send("y_theirs0", y_mine0, swap)
        residual = inputs + total_of([mixed[0], h_far[0], h_near])
    else:
        full = to_all(own_in)
        residual = inputs + total_of(links.scatter_plane(mixed))
    weights = [w.reshape(width, -1) for w in (full, rest)]
    normed_second = (rms_unit(residual) * norm_gains[1]).astype(BF)
    x = after(normed_second, full)

    def run(c, rows, *later):
        chunk_info = after(jnp.concatenate([mine, sources[c]]), *later)
        return expert_chunk(chunk_info, rows, routes_all, router_t, weights)

    if fast:
        near0 = send("near0", x, first)
        both = jnp.stack([x, y])
        both1 = send("both1", both, links.along)
        both3 = send("both3", both, links.against)
        pair0 = jnp.stack([x, near0])
        far0 = send("far0", pair0, second)
        mine0 = jnp.concatenate([pair0, far0])
        theirs0 = send("theirs0", mine0, swap, y_theirs0)
        near1 = send("near1", both1, first)
        both2 = send("both2", both1, links.along)
        pair1 = jnp.stack([both1, near1])
        far1 = send("far1", pair1, second)
        done0 = run(0, [(mine0, None), (theirs0, None), (y_mine0, None), (y_theirs0, None)], pair1, both3)
        past = done0[-1]
        near3 = send("near3", both3, first, pair1)
        mine1 = jnp.concatenate([after(pair1, past), after(far1, past)])
        theirs1 = send("theirs1", mine1, swap, both2)
        swap0 = send("swap0", done0[2], swap, mine1)
        pair3 = jnp.stack([after(both3, past), after(near3, past)])
        far3 = send("far3", pair3, second)
        near2 = send("near2", both2, first, pair3)
        done1 = run(1, [(mine1, 0), (theirs1, 0), (mine1, 1), (theirs1, 1)], pair3, both2)
        past = done1[-1]
        mine3 = jnp.concatenate([after(pair3, past), after(far3, past)])
        pair2 = jnp.stack([after(both2, past), after(near2, past)])
        theirs3 = send("theirs3", mine3, swap)
        far2 = send("far2", pair2, second)
        swap1 = send("swap1", done1[2], swap, mine3)
        d0 = add(after(done0[1], pair2), after(swap0, past)[0])
        done3 = run(3, [(mine3, 0), (theirs3, 0), (mine3, 1), (theirs3, 1)], pair2, d0)
        past = done3[-1]
        mine2 = jnp.concatenate([after(pair2, past), after(far2, past)])
        theirs2 = send("theirs2", mine2, swap)
        swap3 = send("swap3", done3[2], swap, mine2)
        d1 = add(after(done1[1], mine2), after(swap1, past)[0])
        d_far1 = send("d_far1", d1[2:], second)
        d3 = add(after(done3[1], d1), swap3[0])
        d_far3 = send("d_far3", d3[2:], second)
        done2 = run(2, [(mine2, 0), (theirs2, 0), (mine2, 1), (theirs2, 1)], d3)
        past = done2[-1]
        done = [done0, done1, done2, done3]
    else:
        x_all, y_all = links.gather_group(x), links.gather_group(cotangent)
        halves = lambda a, c: [(a[8 * c : 8 * c + 4], None), (a[8 * c + 4 : 8 * c + 8], None)]
        done = [run(c, halves(x_all, c) + halves(y_all, c)) for c in range(chunks)]
        parts = links.scatter_group([(d[1], d[2][0]) for d in done])
    taken, dz, dgu, hid = ([d[k] for d in done] for k in range(3, 7))
    if fast:
        swap2 = send("swap2", done2[2], swap, d_far1, d_far3)
        swaps = [swap0, swap1, swap2, swap3]
        n1, n3 = add(d1[1], d_far1[1]), add(d3[1], after(d_far3, past)[1])
        d_near3 = send("d_near3", n3, first)
        d_near1 = send("d_near1", n1, first, past)
        hid[0] = after(hid[0], n1, n3)
    part_grad = expert_wgrad([(taken, 1, dgu, 2 * F, 2 * QF), (dz, 1, hid, F, QF)], "wgrad_part")

    def give_back(grad, *later):
        got = to_all(after(grad.reshape(n_dp, depth, -1), *later))
        if n_dp == group:
            return got
        return jnp.sum(got.reshape((-1, group) + got.shape[1:]).astype(F32), axis=0).astype(BF)

    got_part = give_back(part_grad)
    if fast:
        d2 = add(after(done2[1], part_grad), swap2[0])
        d_far2 = send("d_far2", d2[2:], second)
        home3 = send("home3", total_of([d3[0], d_far3[0], d_near3]).astype(BF), links.along, part_grad)
        taken[0] = after(taken[0], d2)
    full_grad = expert_wgrad([(taken, 0, dgu, 0, 2 * F)], "wgrad_full")
    if fast:
        d_near2 = send("d_near2", add(d2[1], d_far2[1]), first, full_grad)
        d_far0 = send("d_far0", d0[2:], second, d_far2)
        home2 = send("home2", total_of([d2[0], d_far2[0], d_near2]).astype(BF), links.against)
        m2 = add(after(done[2][0], d_near2), swaps[2][1, ..., :width])
        m_far2 = send("m_far2", m2[2:], second, d_far0)
        h1 = total_of([d1[0], d_far1[0], d_near1, home2]).astype(BF)
        home1 = send("home1", h1, links.against, got_part)
        d_near0 = send("d_near0", add(d0[1], d_far0[1]), first, d_near2)
        m1 = add(after(done[1][0], h1), swaps[1][1, ..., :width])
        m_far1 = send("m_far1", m1[2:], second, h1)
        dz[0] = after(dz[0], m1, h1)
    down_grad = expert_wgrad([(dz, 0, hid, 0, F)], "wgrad_down")
    if fast:
        m_near2 = send("m_near2", add(m2[1], m_far2[1]), first, down_grad)
        parts = [d0[0], d_far0[0], d_near0, home3, after(home1, m_near2)]
        before = (home1,)
    else:
        before = ()
    got_down = give_back(down_grad, got_part, *before)
    got_full = give_back(full_grad, got_down)

    routes_mine = lax.dynamic_slice_in_dim(routes, links.t * own_rows, own_rows, 0)
    residual_grad, branch_grad, second_gain, router_part = residual_gradient(
        parts, normed_second, residual, norm_gains[1:2], router_pad, routes_mine, cotangent
    )
    branch_group = links.gather_plane(branch_grad)
    if fast:
        m_near1 = send("m_near1", add(m1[1], m_far1[1]), first, branch_group)
        m_home2 = send("m_home2", total_of([m2[0], m_far2[0], m_near2]).astype(BF), links.against, branch_grad)
        m3 = add(after(done[3][0], branch_grad), swaps[3][1, ..., :width])
        m_far3 = send("m_far3", m3[2:], second, branch_group)
        before = (m3, got_down)
    else:
        before = ()
    dn1, attention_grad, first_gain = attend_backward(
        heads, after(info, *before), branch_group, normed_group, attention_weights, cosine, sine, qkv, attended, lse, seqs
    )
    attention_mine = lax.psum_scatter(attention_grad, "dp", scatter_dimension=0, tiled=True).astype(F32)
    n_parts = links.scatter_plane(dn1, *([m_home2, m_far3, m_near1] if fast else []))
    first_grad = total_of(n_parts)
    small = jnp.concatenate([router_part, first_gain / norm_gains[0:1], second_gain])
    small = jnp.pad(small, ((0, 6), (0, 0)))
    if fast:
        m0 = add(after(done[0][0], branch_grad), swaps[0][1, ..., :width])
        m_far0 = send("m_far0", m0[2:], second, n_parts[1])
        m_near3 = send("m_near3", add(m3[1], m_far3[1]), first, n_parts[1], got_full)
        m_near0 = send("m_near0", add(m0[1], m_far0[1]), first)
        m_home3 = send("m_home3", total_of([m3[0], m_far3[0], m_near3]).astype(BF), links.along)
        m_home1 = send("m_home1", total_of([m1[0], m_far1[0], m_near1, m_home2]).astype(BF), links.against, dn1)
        out = [m0[0], m_far0[0], m_near0, m_home1, m_home3]
        before = (m_near0, m_near3)
    else:
        out = links.scatter_group([(d[0], d[2][1, ..., :width]) for d in done])
    expert_in_grad, expert_out_grad = unpack_experts(after(got_full, *before), got_down, got_part, experts, group)
    small = links.sum_all(small, *before)
    layer_output = (residual + total_of(out)).astype(BF)

    unit = rms_unit(inputs)
    inner = first_grad * norm_gains[0]
    inverse = lax.rsqrt(jnp.mean(inputs * inputs, axis=-1, keepdims=True) + EPS)
    input_grad = residual_grad + inverse * (inner - unit * jnp.mean(inner * unit, axis=-1, keepdims=True))

    q_wide, kv_wide = heads * GRP * HD, heads * HD
    split = lambda at, size: attention_mine[:, at : at + size].reshape(depth, heads, -1)
    qkv_grad = jnp.transpose(
        jnp.concatenate(
            [split(0, q_wide), split(q_wide, kv_wide), split(q_wide + kv_wide, kv_wide)], axis=2
        ),
        (1, 0, 2),
    )
    out_weight_grad = jnp.transpose(split(q_wide + 2 * kv_wide, q_wide), (1, 2, 0))
    return (
        layer_output,
        input_grad,
        small[E : E + 2],
        jnp.transpose(small[:E]),
        qkv_grad,
        out_weight_grad,
        expert_in_grad,
        jnp.swapaxes(expert_out_grad, 1, 2),
    )


def solution(mesh):
    rows = P(("dp", "tensor"), None)
    return jax.shard_map(
        shards,
        mesh=mesh,
        in_specs=(
            rows,
            rows,
            P("dp", None),
            P("dp", None),
            P(),
            P(),
            P("tensor", "dp", None),
            P("tensor", None, "dp"),
            P("tensor", "dp", None),
            P("tensor", None, "dp"),
        ),
        out_specs=(
            rows,
            rows,
            P(),
            P(),
            P("tensor", "dp", None),
            P("tensor", None, "dp"),
            P("tensor", "dp", None),
            P("tensor", None, "dp"),
        ),
        check_vma=False,
    )
```

```python
import functools

import jax
import jax.numpy as jnp
from jax import lax
from jax.experimental import pallas as pl
from jax.experimental.pallas import tpu as pltpu
from jax.sharding import PartitionSpec as P

HD = 64
GRP = 3
F = 512
QF = F // 4
E = 40
BLK = 256
SLOT = 88
WIN_BLOCKS = 512 // BLK
EPS = 1e-05
THETA = 10000.0
NEG = -1e30
SCALE = HD ** (-0.5)
VMEM = 60 * 1024 * 1024
BF = jnp.bfloat16
COST = pl.CostEstimate(flops=10**6, bytes_accessed=10**4, transcendentals=0)
F32 = jnp.float32


def dot_nn(a, b):
    return lax.dot_general(a, b, (((1,), (0,)), ((), ())), preferred_element_type=F32)


def dot_nt(a, b):
    return lax.dot_general(a, b, (((1,), (1,)), ((), ())), preferred_element_type=F32)


def dot_tn(a, b):
    return lax.dot_general(a, b, (((0,), (0,)), ((), ())), preferred_element_type=F32)


def params(**kw):
    return pltpu.CompilerParams(vmem_limit_bytes=VMEM, **kw)


def whole(shape):
    return pl.BlockSpec(shape, lambda *a: (0,) * len(shape), pipeline_mode=pl.Buffered(1))


class Links:
    def __init__(self, group):
        self.n_dp = lax.axis_size("dp")
        self.n_t = lax.axis_size("tensor")
        self.group = group
        self.fast = self.n_dp == 8 and self.n_t == 4 and group == 8
        self.dp = lax.axis_index("dp")
        self.t = lax.axis_index("tensor")
        if self.fast:
            devices = [(d, t) for d in range(8) for t in range(4)]
            number = lambda d, t: d * 4 + t
            ring = {0: 1, 1: 3, 3: 2, 2: 0}
            self.first = [(number(d, t), number(d, t ^ (2 if d & 1 else 1))) for d, t in devices]
            self.second = [(number(d, t), number(d, t ^ (1 if d & 1 else 2))) for d, t in devices]
            self.swap = [(number(d, t), number(d ^ 1, t)) for d, t in devices]
            self.along = [(number(d, t), number(ring[d >> 1] * 2 + (d & 1), t)) for d, t in devices]
            self.against = [(b, a) for a, b in self.along]
            self.across = [(number(d, t), number(d ^ 6, t)) for d, t in devices]
            self.level = [[(number(d, t), number(d ^ (2 * k), t)) for d, t in devices] for k in range(4)]

    def send(self, label, value, perm, *later):
        value = after(value, *later)
        with jax.named_scope(label):
            return lax.ppermute(value, ("dp", "tensor"), perm)

    def plane_order(self, core):
        one = jnp.where(core == 0, 1, 2)
        return [self.t, self.t ^ one, self.t ^ (3 - one), self.t ^ 3]

    def plane_places(self):
        if not self.fast:
            return jnp.arange(self.n_t, dtype=jnp.int32)
        one = jnp.where((self.dp & 1) == 0, 1, 2)
        diff = jnp.arange(4, dtype=jnp.int32) ^ self.t
        return jnp.where(diff == one, 1, jnp.where(diff == 3 - one, 2, diff)).astype(jnp.int32)

    def gather_plane(self, block, *later):
        if not self.fast:
            return lax.all_gather(block, "tensor", axis=0)
        near = self.send("plane_near", block, self.first, *later)
        pair = jnp.stack([block, near])
        return jnp.concatenate([pair, self.send("plane_far", pair, self.second)])

    def scatter_plane(self, parts, *later):
        if not self.fast:
            rows = parts.reshape((-1,) + parts.shape[2:])
            return [lax.psum_scatter(rows, "tensor", scatter_dimension=0, tiled=True)]
        got = self.send("parts_far", parts[2:], self.second, *later)
        return [parts[0], got[0], self.send("parts_near", add(parts[1], got[1]), self.first)]

    def chunks(self):
        return self.group * self.n_t // 8

    def chunk_sources(self):
        if not self.fast:
            base = (self.dp // self.group) * self.group * self.n_t
            own = [8 * c + jnp.arange(8, dtype=jnp.int32) for c in range(self.chunks())]
            return [base + o for o in own]
        z, core = self.dp >> 1, self.dp & 1
        place = z ^ (z >> 1)
        out = []
        for c in range(4):
            back = (place + 4 - c) & 3
            source = back ^ (back >> 1)
            mine, theirs = self.plane_order(core), self.plane_order(1 - core)
            routes = [(source ^ z) * 4 + t for t in mine] + [((source ^ z) + 4) * 4 + t for t in theirs]
            out.append(jnp.stack(routes).astype(jnp.int32))
        return out

    def groups(self):
        n = self.n_dp // self.group
        return [list(range(g * self.group, (g + 1) * self.group)) for g in range(n)]

    def gather_group(self, block):
        if self.n_dp == self.group:
            return lax.all_gather(block, ("dp", "tensor"), axis=0)
        plane = lax.all_gather(block, "tensor", axis=0)
        return lax.all_gather(plane, "dp", axis=0, axis_index_groups=self.groups()).reshape((-1,) + block.shape)

    def scatter_group(self, pairs):
        rows = jnp.concatenate([half for pair in pairs for half in pair])
        rows = rows.reshape((self.group, -1) + rows.shape[2:])
        total = lax.psum_scatter(rows, "dp", scatter_dimension=0, axis_index_groups=self.groups())
        return [lax.psum_scatter(total, "tensor", scatter_dimension=0, tiled=True)]

    def sum_all(self, value, *later):
        if not self.fast:
            return lax.psum(value, ("dp", "tensor"))
        for perm in (self.swap, self.first, self.second):
            value = value + self.send("small", value, perm)
        value = after(value, *later)
        for perm in self.level[1:3]:
            value = value + self.send("small", value, perm)
        return value


def after(value, *earlier):
    return lax.optimization_barrier((value,) + earlier)[0] if earlier else value


def total_of(parts):
    total = parts[0].astype(F32)
    for part in parts[1:]:
        total = total + part.astype(F32)
    return total


def add(a, b):
    return (a.astype(F32) + b.astype(F32)).astype(a.dtype)


def pack_attention_kernel(heads, qkv_ref, out_ref, packed_ref):
    q_wide, kv_wide = heads * GRP * HD, heads * HD
    for h in range(heads):
        one = qkv_ref[h]
        packed_ref[:, h * GRP * HD : (h + 1) * GRP * HD] = one[:, : GRP * HD]
        packed_ref[:, q_wide + h * HD : q_wide + (h + 1) * HD] = one[:, GRP * HD : (GRP + 1) * HD]
        at = q_wide + kv_wide + h * HD
        packed_ref[:, at : at + HD] = one[:, (GRP + 1) * HD :]
        at = q_wide + 2 * kv_wide + h * GRP * HD
        packed_ref[:, at : at + GRP * HD] = out_ref[h].astype(F32).T.astype(BF)


def pack_attention(qkv_weight, out_weight):
    heads, depth, _ = qkv_weight.shape
    return pl.pallas_call(
        functools.partial(pack_attention_kernel, heads),
        out_shape=jax.ShapeDtypeStruct((depth, heads * (2 * GRP + 2) * HD), BF),
        compiler_params=params(),
        name="pack_attention",
    )(qkv_weight, out_weight)


def attention_places(links):
    if not links.fast:
        return jnp.arange(links.n_dp, dtype=jnp.int32)
    z, core = links.dp >> 1, links.dp & 1
    near = [(z ^ k) * 2 for k in range(4)]
    return jnp.stack([n + core for n in near] + [n + 1 - core for n in near]).astype(jnp.int32)


def pack_kernel(gate_ref, up_ref, part_ref, down_ref, packed_ref):
    packed_ref[0, :, :QF] = gate_ref[0]
    packed_ref[0, :, QF : 2 * QF] = up_ref[0]
    packed_ref[0, :, 2 * QF : 3 * QF] = part_ref[0]
    packed_ref[0, :, 3 * QF :] = down_ref[0]


def pack_experts(expert_in, expert_out_t, group, n_dp):
    depth = expert_in.shape[1]
    of = lambda d: d % group
    return pl.pallas_call(
        pack_kernel,
        grid=(n_dp,),
        in_specs=[
            pl.BlockSpec((1, depth, QF), lambda d: (group + of(d) // 4, 0, of(d) % 4)),
            pl.BlockSpec((1, depth, QF), lambda d: (group + of(d) // 4, 0, 4 + of(d) % 4)),
            pl.BlockSpec((1, depth, QF), lambda d: (group + of(d) // 4, 0, of(d) % 4)),
            pl.BlockSpec((1, depth, F), lambda d: (of(d), 0, 0)),
        ],
        out_specs=pl.BlockSpec((1, depth, 3 * QF + F), lambda d: (d, 0, 0)),
        out_shape=jax.ShapeDtypeStruct((n_dp, depth, 3 * QF + F), BF),
        compiler_params=params(),
        name="pack_experts",
    )(expert_in, expert_in, expert_out_t, expert_out_t)


def unpack_kernel(group, full_ref, down_ref, part_ref, in_ref, out_ref):
    e = pl.program_id(0)

    @pl.when(e < group)
    def _():
        in_ref[0] = full_ref[0].astype(F32)
        out_ref[0] = down_ref[0].astype(F32)

    @pl.when(e >= group)
    def _():
        for q in range(4):
            part = part_ref[(e - group) * 4 + q].astype(F32)
            in_ref[0, :, q * QF : (q + 1) * QF] = part[:, :QF]
            in_ref[0, :, F + q * QF : F + (q + 1) * QF] = part[:, QF : 2 * QF]
            out_ref[0, :, q * QF : (q + 1) * QF] = part[:, 2 * QF :]


def unpack_experts(full, down, part, experts, group):
    depth = full.shape[1]
    first = lambda e: (jnp.minimum(e, group - 1), 0, 0)
    return pl.pallas_call(
        functools.partial(unpack_kernel, group),
        grid=(experts,),
        in_specs=[
            pl.BlockSpec((1, depth, 2 * F), first),
            pl.BlockSpec((1, depth, F), first),
            whole(part.shape),
        ],
        out_specs=(
            pl.BlockSpec((1, depth, 2 * F), lambda e: (e, 0, 0)),
            pl.BlockSpec((1, depth, F), lambda e: (e, 0, 0)),
        ),
        out_shape=(
            jax.ShapeDtypeStruct((experts, depth, 2 * F), F32),
            jax.ShapeDtypeStruct((experts, depth, F), F32),
        ),
        compiler_params=params(),
        name="unpack_experts",
    )(full, down, part)


def expert_kernel(
    info_ref, xa_ref, xb_ref, ya_ref, yb_ref, routes_ref, router_ref, full_ref, rest_ref,
    ma_ref, da_ref, theirs_ref, taken_ref, dz_ref, dgu_ref, hid_ref,
):
    step = pl.program_id(0)
    first, second = info_ref[0], info_ref[1]
    expert_id = lax.broadcasted_iota(jnp.int32, (E, BLK), 0)
    slot_id = lax.broadcasted_iota(jnp.int32, (SLOT, BLK), 0)
    upto = (
        lax.broadcasted_iota(jnp.int32, (BLK, BLK), 0) <= lax.broadcasted_iota(jnp.int32, (BLK, BLK), 1)
    ).astype(BF)
    row_id = lax.broadcasted_iota(jnp.int32, (8, BLK), 0)
    picks, slot_gates, taken, dz = [], ([], []), ([], []), ([], [])
    for b in range(4):
        x = (xa_ref if b < 2 else xb_ref)[b % 2].reshape(BLK, -1)
        y = (ya_ref if b < 2 else yb_ref)[b % 2].reshape(BLK, -1)
        routes = routes_ref[info_ref[2 + step * 2 + b % 2 + (0 if b < 2 else 4)]]
        logits = dot_nt(router_ref[...], x)
        member = expert_id == routes[0:1]
        for k in range(1, 8):
            member = member | (expert_id == routes[k : k + 1])
        masked = jnp.where(member, logits, NEG)
        shifted = jnp.exp(masked - jnp.max(masked, axis=0, keepdims=True))
        shifted = jnp.where(member, shifted, 0.0)
        gates = shifted / jnp.sum(shifted, axis=0, keepdims=True)
        member = member.astype(F32)
        rows = []
        for e in (first, second):
            here = expert_id == e
            rows.append(
                (
                    jnp.sum(jnp.where(here, gates, 0.0), axis=0, keepdims=True),
                    jnp.sum(jnp.where(here, member, 0.0), axis=0, keepdims=True),
                )
            )
        both = jnp.where(row_id == 0, rows[0][1], jnp.where(row_id == 1, rows[1][1], 0.0))
        counts = dot_nn(both.astype(BF), upto).astype(jnp.int32)
        pick = []
        for j in range(2):
            spot = jnp.where(rows[j][1] > 0.0, counts[j : j + 1] - 1, -1)
            hot = (slot_id == spot).astype(F32)
            slot_gates[j].append(jnp.sum(hot * rows[j][0], axis=1, keepdims=True))
            pick.append(hot)
        pick = jnp.concatenate(pick, axis=0).astype(BF)
        picks.append(pick)
        got = dot_nn(pick, x)
        taken[0].append(got[:SLOT])
        taken[1].append(got[SLOT:])
        got = dot_nn(pick, y)
        dz[0].append(got[:SLOT])
        dz[1].append(got[SLOT:])
    sends, backs = [], []
    for j in range(2):
        width = F if j == 0 else QF
        in_at = 0 if j == 0 else 2 * F
        rows = jnp.concatenate(taken[j], axis=0).astype(BF)
        grads = jnp.concatenate(dz[j], axis=0).astype(BF)
        gate = jnp.concatenate(slot_gates[j], axis=0)
        taken_ref[0, j] = rows
        dz_ref[0, j] = grads
        w_in = full_ref[...] if j == 0 else rest_ref[:, : 2 * QF]
        w_out = rest_ref[:, 3 * QF :] if j == 0 else rest_ref[:, 2 * QF : 3 * QF]
        gate_up = dot_nn(rows, w_in)
        gate_part, up_part = gate_up[:, :width], gate_up[:, width:]
        sig = 1.0 / (1.0 + jnp.exp(-gate_part))
        silu = gate_part * sig
        hidden = silu * up_part
        scaled = (gate * hidden).astype(BF)
        hid_at = 0 if j == 0 else F
        hid_ref[0, :, hid_at : hid_at + width] = scaled
        sends.append(dot_nt(scaled, w_out))
        raw = dot_nn(grads, w_out)
        dgate = jnp.sum(hidden.astype(BF).astype(F32) * raw, axis=1, keepdims=True)
        dhid = gate * raw
        dgu = jnp.concatenate(
            [dhid * up_part * (sig * (1.0 + gate_part * (1.0 - sig))), dhid * silu], axis=1
        ).astype(BF)
        dgu_ref[0, :, in_at : in_at + 2 * width] = dgu
        back = dot_nt(dgu, w_in)
        lane = lax.broadcasted_iota(jnp.int32, (1, 128), 1)
        e = first if j == 0 else second
        high = dgate.astype(BF).astype(F32)
        extra = jnp.where(lane == e, high, 0.0) + jnp.where(lane == e + 64, dgate - high, 0.0)
        backs.append(jnp.concatenate([back, extra], axis=1))
    for b in range(4):
        at = slice(b * SLOT, (b + 1) * SLOT)
        for kind, values in enumerate((backs, sends)):
            stacked = jnp.concatenate([values[0][at], values[1][at]], axis=0).astype(BF)
            summed = dot_tn(picks[b], stacked).astype(BF)
            if b < 2:
                (da_ref, ma_ref)[kind][b] = summed
            else:
                theirs_ref[kind, b - 2, :, : summed.shape[1]] = summed


def stepped(shape):
    return pl.BlockSpec((1,) + shape[1:], lambda s, *_: (s,) + (0,) * (len(shape) - 1))


def expert_chunk(info, rows, routes, router_t, weights):
    width = rows[0][0].shape[-1]
    shape = jax.ShapeDtypeStruct
    half = pl.BlockSpec((2, BLK, width), lambda s, i: (s, 0, 0))

    def given(array, column):
        if column is None:
            return half
        return pl.BlockSpec((2, 1, BLK, width), lambda s, i: (s, column, 0, 0))

    slots = 4 * SLOT
    kept = [
        shape((2, 2, slots, width), BF),
        shape((2, 2, slots, width), BF),
        shape((2, slots, 2 * F + 2 * QF), BF),
        shape((2, slots, F + QF), BF),
    ]
    return pl.pallas_call(
        expert_kernel,
        grid_spec=pltpu.PrefetchScalarGridSpec(
            num_scalar_prefetch=1,
            grid=(2,),
            in_specs=[given(*r) for r in rows] + [whole(a.shape) for a in (routes, router_t, *weights)],
            out_specs=[
                half,
                pl.BlockSpec((2, BLK, width + 128), lambda s, i: (s, 0, 0)),
                pl.BlockSpec((2, 2, BLK, width + 128), lambda s, i: (0, s, 0, 0)),
            ]
            + [stepped(s.shape) for s in kept],
        ),
        out_shape=[
            shape((4, BLK, width), BF),
            shape((4, BLK, width + 128), BF),
            shape((2, 4, BLK, width + 128), BF),
        ]
        + kept,
        compiler_params=params(),
        cost_estimate=pl.CostEstimate(flops=30 * 10**9, bytes_accessed=45 * 10**6, transcendentals=10**6),
        name="experts",
    )(info, *[r[0] for r in rows], routes, router_t, *weights)


def wgrad_kernel(chunks, pairs, *refs):
    out_ref = refs[-1]
    flat = lambda v: v.reshape((-1, v.shape[-1]))
    at = 0
    for p in range(pairs):
        left, right = refs[2 * p * chunks : (2 * p + 1) * chunks], refs[(2 * p + 1) * chunks : (2 * p + 2) * chunks]
        total = dot_tn(flat(left[0][...]), flat(right[0][...]))
        for l, r in zip(left[1:], right[1:]):
            total = total + dot_tn(flat(l[...]), flat(r[...]))
        out_ref[:, at : at + total.shape[1]] = total.astype(BF)
        at += total.shape[1]


def expert_wgrad(pairs, name):
    width = pairs[0][0][0].shape[-1]
    chunks = len(pairs[0][0])
    tile = 256
    specs, operands, columns = [], [], 0
    for left, j, right, at, size in pairs:
        rows = left[0].shape[2]
        specs += [pl.BlockSpec((2, 1, rows, tile), lambda k, j=j: (0, j, 0, k))] * chunks
        specs += [
            pl.BlockSpec((2, rows, size), lambda k, b=at // size: (0, 0, b), pipeline_mode=pl.Buffered(1))
        ] * chunks
        operands += list(left) + list(right)
        columns += size
    return pl.pallas_call(
        functools.partial(wgrad_kernel, chunks, len(pairs)),
        grid=(width // tile,),
        in_specs=specs,
        out_specs=pl.BlockSpec((tile, columns), lambda k: (k, 0)),
        out_shape=jax.ShapeDtypeStruct((width, columns), BF),
        compiler_params=params(),
        cost_estimate=COST,
        name=name,
    )(*operands)


def swap_halves(values):
    width = values.shape[1]
    lane = lax.broadcasted_iota(jnp.int32, values.shape, 1)
    up = pltpu.roll(values, width - HD // 2, 1)
    down = pltpu.roll(values, HD // 2, 1)
    return jnp.where((lane & (HD - 1)) < HD // 2, up, down)


def spread(table, width):
    return jnp.concatenate([table] * (width // 128), axis=1)


def allowed_mask(starts, block, window):
    first = (block - window + 1) * BLK
    shape = (BLK, window * BLK)
    query = block * BLK + lax.broadcasted_iota(jnp.int32, shape, 0)
    key = first + lax.broadcasted_iota(jnp.int32, shape, 1)
    begin = jnp.zeros(shape, jnp.int32)
    for s in starts:
        begin = jnp.where(query >= s, s, begin)
    return (key >= begin) & (key <= query)


def over_windows(block, blocks, body):
    for w in range(1, min(WIN_BLOCKS + 1, blocks) + 1):
        last = w == WIN_BLOCKS + 1
        pl.when((block >= w - 1) if last else (block == w - 1))(functools.partial(body, w))


def heads_to_rows(values, first):
    return jnp.concatenate([values[:, (first + g) * HD : (first + g + 1) * HD] for g in range(GRP)], axis=0)


def rows_to_heads(values):
    return [values[g * BLK : (g + 1) * BLK] for g in range(GRP)]


def attend_kernel(heads, blocks, seqs, pieces, info_ref, n1_ref, cos_ref, sin_ref, *refs):
    out_ref, qkv_ref, o_ref, lse_ref, w_ref = refs[pieces:]
    i = pl.program_id(0)

    @pl.when(i == 0)
    def _():
        each = [ref.at[p] for ref in refs[:pieces] for p in range(ref.shape[0])]
        depth = w_ref.shape[0] // len(each)
        for k, piece in enumerate(each):
            at = pl.multiple_of(info_ref[blocks + seqs + k] * depth, depth)
            w_ref[pl.ds(at, depth), :] = piece[:depth]

    q_wide, kv_wide = heads * GRP * HD, heads * HD
    rot_wide, qkv_wide = q_wide + kv_wide, q_wide + 2 * kv_wide
    projected = dot_nn(n1_ref[0], w_ref[:, :qkv_wide])
    turning = projected[:, :rot_wide]
    turned = turning * spread(cos_ref[...], rot_wide) + swap_halves(turning) * spread(sin_ref[...], rot_wide)
    rows = pl.ds(pl.multiple_of(i * BLK, BLK), BLK)
    queries = (turned[:, :q_wide].astype(BF).astype(F32) * SCALE).astype(BF)
    qkv_ref[rows, :q_wide] = queries
    qkv_ref[rows, q_wide:rot_wide] = turned[:, q_wide:].astype(BF)
    qkv_ref[rows, rot_wide:] = projected[:, rot_wide:].astype(BF)
    starts = [info_ref[blocks + s] for s in range(seqs)]

    def attend(window):
        keep = allowed_mask(starts, i, window)
        keys = pl.ds(pl.multiple_of((i - window + 1) * BLK, BLK), window * BLK)
        lane = lax.broadcasted_iota(jnp.int32, (BLK, 128), 1)
        lse_all = jnp.zeros((BLK, 128), F32)
        attended = []
        for h in range(heads):
            k_rows = qkv_ref[keys, q_wide + h * HD : q_wide + (h + 1) * HD]
            v_rows = qkv_ref[keys, rot_wide + h * HD : rot_wide + (h + 1) * HD]
            scores = dot_nt(heads_to_rows(queries, h * GRP), k_rows)
            for g in range(GRP):
                part = jnp.where(keep, scores[g * BLK : (g + 1) * BLK], NEG)
                top = jnp.max(part, axis=1, keepdims=True)
                shifted = jnp.exp(part - top)
                total = jnp.sum(shifted, axis=1, keepdims=True)
                probability = (shifted * (1.0 / total)).astype(BF)
                attended.append(dot_nn(probability, v_rows).astype(BF))
                lse_all = jnp.where(lane == h * GRP + g, top + jnp.log(total), lse_all)
        lse_ref[...] = lse_all
        attended = jnp.concatenate(attended, axis=1)
        o_ref[...] = attended
        out_ref[0] = dot_nt(attended, w_ref[:, qkv_wide:]).astype(BF)

    over_windows(i, blocks, attend)


def attend_forward(heads, info, normed, pieces, cosine, sine, seqs):
    blocks, _, width = normed.shape
    rows = blocks * BLK
    q_wide = heads * GRP * HD
    qkv_wide = q_wide + 2 * heads * HD
    shape = jax.ShapeDtypeStruct
    weights = (width, pieces[0].shape[-1])
    return pl.pallas_call(
        functools.partial(attend_kernel, heads, blocks, seqs, len(pieces)),
        grid_spec=pltpu.PrefetchScalarGridSpec(
            num_scalar_prefetch=1,
            grid=(blocks,),
            in_specs=[
                pl.BlockSpec((1, BLK, width), lambda i, info: (info[i], 0, 0)),
                pl.BlockSpec((BLK, 128), lambda i, info: (i, 0)),
                pl.BlockSpec((BLK, 128), lambda i, info: (i, 0)),
            ]
            + [whole(p.shape) for p in pieces],
            out_specs=[
                pl.BlockSpec((1, BLK, width), lambda i, info: (info[i], 0, 0)),
                whole((rows, qkv_wide)),
                pl.BlockSpec((BLK, q_wide), lambda i, info: (i, 0)),
                pl.BlockSpec((BLK, 128), lambda i, info: (i, 0)),
                whole(weights),
            ],
        ),
        out_shape=[
            shape((blocks, BLK, width), BF),
            shape((rows, qkv_wide), BF),
            shape((rows, q_wide), BF),
            shape((rows, 128), F32),
            shape(weights, BF),
        ],
        compiler_params=params(),
        cost_estimate=COST,
        name="attend",
    )(info, normed, cosine, sine, *pieces)


def attend_back_kernel(
    heads,
    blocks,
    seqs,
    info_ref,
    da_ref,
    n1_ref,
    w_ref,
    cos_ref,
    sin_ref,
    qkv_ref,
    o_ref,
    lse_ref,
    dn1_ref,
    dw_ref,
    gain_ref,
    acc_ref,
    dq_ref,
    dkv_ref,
):
    step = pl.program_id(0)
    q_wide, kv_wide = heads * GRP * HD, heads * HD
    rot_wide, qkv_wide = q_wide + kv_wide, q_wide + 2 * kv_wide
    starts = [info_ref[blocks + s] for s in range(seqs)]

    @pl.when(step == 0)
    def _():
        acc_ref[...] = jnp.zeros_like(acc_ref)
        dkv_ref[...] = jnp.zeros_like(dkv_ref)
        gain_ref[...] = jnp.zeros_like(gain_ref)

    @pl.when(step < blocks)
    def _():
        i = step
        da = da_ref[0]
        w_out = w_ref[:, qkv_wide:]
        grad = dot_nn(da, w_out).astype(BF)
        acc_ref[:, qkv_wide:] += dot_tn(da, o_ref[...])
        rows = pl.ds(pl.multiple_of(i * BLK, BLK), BLK)
        queries = qkv_ref[rows, :q_wide]
        lse = lse_ref[...]

        def back(window):
            keep = allowed_mask(starts, i, window)
            keys = pl.ds(pl.multiple_of((i - window + 1) * BLK, BLK), window * BLK)
            for h in range(heads):
                k_rows = qkv_ref[keys, q_wide + h * HD : q_wide + (h + 1) * HD]
                v_rows = qkv_ref[keys, rot_wide + h * HD : rot_wide + (h + 1) * HD]
                stacked_q = heads_to_rows(queries, h * GRP)
                stacked_g = heads_to_rows(grad, h * GRP)
                scores = dot_nt(stacked_q, k_rows)
                dprob = dot_nt(stacked_g, v_rows)
                probs, dscores = [], []
                for g in range(GRP):
                    at = slice(g * BLK, (g + 1) * BLK)
                    one = h * GRP + g
                    prob = jnp.where(keep, jnp.exp(scores[at] - lse[:, one : one + 1]), 0.0)
                    both = prob * dprob[at]
                    inner = jnp.sum(both, axis=1, keepdims=True)
                    dscores.append((both - prob * inner).astype(BF))
                    probs.append(prob.astype(BF))
                probs = jnp.concatenate(probs, axis=0)
                dscores = jnp.concatenate(dscores, axis=0)
                dq = dot_nn(dscores, k_rows) * SCALE
                dq_ref[rows, h * GRP * HD : (h + 1) * GRP * HD] = jnp.concatenate(rows_to_heads(dq), axis=1)
                dkv_ref[h, keys, :HD] += dot_tn(dscores, stacked_q)
                dkv_ref[h, keys, HD:] += dot_tn(probs, stacked_g)

        over_windows(i, blocks, back)

    @pl.when(step >= blocks)
    def _():
        j = step - blocks
        rows = pl.ds(pl.multiple_of(j * BLK, BLK), BLK)
        dk = [dkv_ref[h, rows, :HD] for h in range(heads)]
        dv = [dkv_ref[h, rows, HD:] for h in range(heads)]
        turned = jnp.concatenate([dq_ref[rows, :]] + dk, axis=1)
        turned = turned * spread(cos_ref[...], rot_wide) - swap_halves(turned) * spread(sin_ref[...], rot_wide)
        dqkv = jnp.concatenate([turned] + dv, axis=1).astype(BF)
        n1 = n1_ref[0]
        acc_ref[:, :qkv_wide] += dot_tn(n1, dqkv)
        dn1 = dot_nt(dqkv, w_ref[:, :qkv_wide])
        gain_ref[...] += jnp.sum(dn1 * n1.astype(F32), axis=0, keepdims=True)
        dn1_ref[0] = dn1.astype(BF)

    @pl.when(step == 2 * blocks - 1)
    def _():
        dw_ref[...] = acc_ref[...].astype(BF)


def attend_backward(heads, info, da, normed, weights, cosine, sine, qkv, attended, lse, seqs):
    blocks, _, width = normed.shape
    rows = blocks * BLK
    q_wide = heads * GRP * HD
    shape = jax.ShapeDtypeStruct
    early = lambda i: jnp.minimum(i, blocks - 1)
    late = lambda i: jnp.maximum(i - blocks, 0)
    return pl.pallas_call(
        functools.partial(attend_back_kernel, heads, blocks, seqs),
        grid_spec=pltpu.PrefetchScalarGridSpec(
            num_scalar_prefetch=1,
            grid=(2 * blocks,),
            in_specs=[
                pl.BlockSpec((1, BLK, width), lambda i, info: (info[early(i)], 0, 0)),
                pl.BlockSpec((1, BLK, width), lambda i, info: (info[late(i)], 0, 0)),
                whole(weights.shape),
                pl.BlockSpec((BLK, 128), lambda i, info: (late(i), 0)),
                pl.BlockSpec((BLK, 128), lambda i, info: (late(i), 0)),
                whole(qkv.shape),
                pl.BlockSpec((BLK, q_wide), lambda i, info: (early(i), 0)),
                pl.BlockSpec((BLK, 128), lambda i, info: (early(i), 0)),
            ],
            out_specs=[
                pl.BlockSpec((1, BLK, width), lambda i, info: (info[late(i)], 0, 0)),
                whole(weights.shape),
                whole((1, width)),
            ],
            scratch_shapes=[
                pltpu.VMEM(weights.shape, F32),
                pltpu.VMEM((rows, q_wide), F32),
                pltpu.VMEM((heads, rows, 2 * HD), F32),
            ],
        ),
        out_shape=[shape((blocks, BLK, width), BF), shape(weights.shape, BF), shape((1, width), F32)],
        compiler_params=params(),
        cost_estimate=COST,
        name="attend_back",
    )(info, da, normed, weights, cosine, sine, qkv, attended, lse)


def residual_kernel(parts, *refs):
    part_refs = refs[:parts]
    n2_ref, h_ref, gain_ref, router_ref, routes_ref, cot_ref, dh_ref, da_ref, dgain_ref, drouter_ref = refs[parts:]
    width = n2_ref.shape[1]
    total = total_of([r[...] for r in part_refs])
    dn2 = total[:, :width]
    dgate = total[:, width:]
    dgate = dgate + pltpu.roll(dgate, 64, 1)
    n2 = n2_ref[...]
    logits = dot_nt(n2, router_ref[...])
    lane = lax.broadcasted_iota(jnp.int32, logits.shape, 1)
    routes = routes_ref[...]
    member = lane == routes[:, 0:1]
    for k in range(1, 8):
        member = member | (lane == routes[:, k : k + 1])
    masked = jnp.where(member, logits, NEG)
    shifted = jnp.where(member, jnp.exp(masked - jnp.max(masked, axis=1, keepdims=True)), 0.0)
    gates = shifted / jnp.sum(shifted, axis=1, keepdims=True)
    dgate = jnp.where(member, dgate, 0.0)
    dlogit = gates * (dgate - jnp.sum(gates * dgate, axis=1, keepdims=True))
    high = dlogit.astype(BF)
    low = (dlogit - high.astype(F32)).astype(BF)
    dn2 = dn2 + dot_nn(high, router_ref[...]) + dot_nn(low, router_ref[...])
    drouter_ref[...] = (dot_tn(high, n2) + dot_tn(low, n2))[:E]
    h = h_ref[...]
    inverse = lax.rsqrt(jnp.mean(h * h, axis=1, keepdims=True) + EPS)
    unit = h * inverse
    dgain_ref[...] = jnp.sum(dn2 * unit, axis=0, keepdims=True)
    inner = dn2 * gain_ref[...]
    dh = cot_ref[...].astype(F32) + inverse * (inner - unit * jnp.mean(inner * unit, axis=1, keepdims=True))
    dh_ref[...] = dh
    da_ref[...] = dh.astype(BF)


def residual_gradient(parts, n2, h, gain, router_pad, routes, cotangent):
    rows, width = n2.shape
    shape = jax.ShapeDtypeStruct
    return pl.pallas_call(
        functools.partial(residual_kernel, len(parts)),
        out_shape=[
            shape((rows, width), F32),
            shape((rows, width), BF),
            shape((1, width), F32),
            shape((E, width), F32),
        ],
        compiler_params=params(),
        cost_estimate=COST,
        name="residual_gradient",
    )(*parts, n2, h, gain, router_pad, routes, cotangent)


def rms_unit(values):
    return values * lax.rsqrt(jnp.mean(values * values, axis=-1, keepdims=True) + EPS)


def rope_tables(starts, rows):
    index = jnp.arange(rows, dtype=jnp.int32)
    begin = jnp.max(jnp.where(index[:, None] >= starts[None, :], starts[None, :], 0), axis=1)
    position = (index - begin).astype(F32)
    halfway = HD // 2
    frequency = THETA ** (-(jnp.arange(halfway, dtype=F32) * 2.0 / HD))
    angles = position[:, None] * frequency[None, :]
    cosine, sine = jnp.cos(angles), jnp.sin(angles)
    return (
        jnp.concatenate([cosine] * 4, axis=1),
        jnp.concatenate([-sine, sine, -sine, sine], axis=1),
    )


def shards(tokens, cotangent, lengths, routes, norm_gains, router_weight, qkv_weight, out_weight, expert_in, expert_out):
    own_rows, width = tokens.shape
    group_rows = routes.shape[0]
    heads = qkv_weight.shape[0]
    experts, depth, _ = expert_in.shape
    group = experts * 4 // 5
    n_dp = lax.axis_size("dp")
    links = Links(group)
    fast = links.fast
    send, first, second = links.send, (links.first if fast else None), (links.second if fast else None)
    rank = links.dp % group
    own_expert = links.t * experts + rank
    part_expert = links.t * experts + group + rank // 4
    seqs = lengths.shape[1]
    blocks = group_rows // own_rows
    inputs = tokens.astype(F32)
    expert_out_t = jnp.swapaxes(expert_out, 1, 2)
    starts = jnp.cumsum(lengths[0]) - lengths[0]
    cosine, sine = rope_tables(starts, group_rows)
    info = jnp.concatenate([links.plane_places(), starts.astype(jnp.int32), attention_places(links)])
    router_t = jnp.transpose(router_weight)
    router_pad = jnp.pad(router_t, ((0, 128 - E), (0, 0)))
    mine = jnp.stack([own_expert, part_expert]).astype(jnp.int32)
    sources = links.chunk_sources()
    chunks = links.chunks()
    to_all = lambda a: lax.all_to_all(a, "dp", 0, 0)

    shard = pack_attention(qkv_weight, out_weight)
    normed_first = (rms_unit(inputs) * norm_gains[0]).astype(BF)
    packed = pack_experts(expert_in, expert_out_t, group, n_dp)
    own_in = expert_in[:group] if n_dp == group else jnp.concatenate([expert_in[:group]] * (n_dp // group))
    routes_t = jnp.transpose(routes)
    by_block = lambda r: jnp.transpose(r.reshape(-1, 8, blocks, own_rows), (0, 2, 1, 3)).reshape(-1, 8, own_rows)
    if fast:
        y, swap = cotangent, links.swap
        routes_rows = jnp.pad(routes_t.astype(BF), ((0, 8), (0, 0)))
        shard = jnp.concatenate([shard, routes_rows])
        pieces = [send("pieces", shard, links.level[k]) for k in range(1, 4)]
        near = send("near", normed_first, first, shard)
        pair = jnp.stack([normed_first, near])
        far = send("far", pair, second)

        pieces_mine = jnp.stack([shard] + pieces)
        pieces_theirs = send("pieces_theirs", pieces_mine, swap)
        y_near0 = send("y_near0", y, first, far)
        rest = to_all(after(packed, pieces_mine))
        normed_group = jnp.concatenate([pair, far])
        y_pair0 = jnp.stack([y, y_near0])
        y_far0 = send("y_far0", y_pair0, second)
        attend_pieces = [pieces_mine, pieces_theirs]
        routes_all = jnp.concatenate([pieces_mine[:, depth : depth + 8], pieces_theirs[:, depth : depth + 8]])
        routes_all = by_block(routes_all).astype(jnp.int32)
        before = (rest, y_far0)
    else:
        normed_group = links.gather_plane(normed_first)
        attend_pieces = [lax.all_gather(shard, "dp", axis=0)]
        rest = to_all(packed)
        routes_all = by_block(lax.all_gather(routes_t, "dp", axis=0))
        before = (packed,)
    mixed, qkv, attended, lse, attention_weights = attend_forward(
        heads, after(info, *before), normed_group, attend_pieces, cosine, sine, seqs
    )
    if fast:
        full = to_all(after(own_in, rest))
        h_far = send("h_far", mixed[2:], second)
        h_near = send("h_near", add(mixed[1], h_far[1]), first)
        y_mine0 = jnp.concatenate([y_pair0, after(y_far0, mixed)])
        y_theirs0 = send("y_theirs0", y_mine0, swap)
        residual = inputs + total_of([mixed[0], h_far[0], h_near])
    else:
        full = to_all(own_in)
        residual = inputs + total_of(links.scatter_plane(mixed))
    weights = [w.reshape(width, -1) for w in (full, rest)]
    normed_second = (rms_unit(residual) * norm_gains[1]).astype(BF)
    x = after(normed_second, full)

    def run(c, rows, *later):
        chunk_info = after(jnp.concatenate([mine, sources[c]]), *later)
        return expert_chunk(chunk_info, rows, routes_all, router_t, weights)

    if fast:
        both = jnp.stack([x, y])
        near0 = send("near0", x, first, both)
        both1 = send("both1", both, links.along)
        both3 = send("both3", both, links.against)
        pair0 = jnp.stack([x, near0])
        far0 = send("far0", pair0, second)
        mine0 = jnp.concatenate([pair0, far0])
        near1 = send("near1", both1, first)
        theirs0 = send("theirs0", mine0, swap, y_theirs0, near1)
        both2 = send("both2", both1, links.along)
        pair1 = jnp.stack([both1, near1])
        far1 = send("far1", pair1, second)
        done0 = run(0, [(mine0, None), (theirs0, None), (y_mine0, None), (y_theirs0, None)], pair1)
        past = done0[-1]
        near3 = send("near3", both3, first, past)
        mine1 = jnp.concatenate([after(pair1, past), after(far1, past)])
        theirs1 = send("theirs1", mine1, swap, both3)
        swap0 = send("swap0", done0[2], swap, mine1)
        pair3 = jnp.stack([after(both3, past), after(near3, past)])
        far3 = send("far3", pair3, second)

        done1 = run(1, [(mine1, 0), (theirs1, 0), (mine1, 1), (theirs1, 1)], pair3)
        past = done1[-1]
        near2 = send("near2", both2, first, past)
        mine3 = jnp.concatenate([after(pair3, past), after(far3, past)])
        pair2 = jnp.stack([after(both2, past), after(near2, past)])
        theirs3 = send("theirs3", mine3, swap, both2)
        far2 = send("far2", pair2, second)
        swap1 = send("swap1", done1[2], swap, mine3)
        d0 = add(after(done0[1], pair2), after(swap0, past)[0])
        done3 = run(3, [(mine3, 0), (theirs3, 0), (mine3, 1), (theirs3, 1)], pair2, d0)
        past = done3[-1]
        mine2 = jnp.concatenate([after(pair2, past), after(far2, past)])
        theirs2 = send("theirs2", mine2, swap)
        swap3 = send("swap3", done3[2], swap, mine2)
        d1 = add(after(done1[1], mine2), after(swap1, past)[0])
        d_far1 = send("d_far1", d1[2:], second)
        d3 = add(after(done3[1], d1), swap3[0])
        d_far3 = send("d_far3", d3[2:], second)
        done2 = run(2, [(mine2, 0), (theirs2, 0), (mine2, 1), (theirs2, 1)], d3)
        past = done2[-1]
        done = [done0, done1, done2, done3]
    else:
        x_all, y_all = links.gather_group(x), links.gather_group(cotangent)
        halves = lambda a, c: [(a[8 * c : 8 * c + 4], None), (a[8 * c + 4 : 8 * c + 8], None)]
        done = [run(c, halves(x_all, c) + halves(y_all, c)) for c in range(chunks)]
        parts = links.scatter_group([(d[1], d[2][0]) for d in done])
    taken, dz, dgu, hid = ([d[k] for d in done] for k in range(3, 7))
    if fast:
        swap2 = send("swap2", done2[2], swap, d_far1, d_far3)
        swaps = [swap0, swap1, swap2, swap3]
        n1, n3 = add(d1[1], d_far1[1]), add(d3[1], after(d_far3, past)[1])
        d_near3 = send("d_near3", n3, first)
        d_near1 = send("d_near1", n1, first, past)
        hid[0] = after(hid[0], n1, n3)
    part_grad = expert_wgrad([(taken, 1, dgu, 2 * F, 2 * QF), (dz, 1, hid, F, QF)], "wgrad_part")

    def give_back(grad, *later):
        got = to_all(after(grad.reshape(n_dp, depth, -1), *later))
        if n_dp == group:
            return got
        return jnp.sum(got.reshape((-1, group) + got.shape[1:]).astype(F32), axis=0).astype(BF)

    if fast:
        d2 = add(after(done2[1], part_grad), swap2[0])
        d_far2 = send("d_far2", d2[2:], second)
        home3 = send("home3", total_of([d3[0], d_far3[0], d_near3]).astype(BF), links.along, part_grad)
        taken[0] = after(taken[0], d2)
    got_part = give_back(part_grad)
    full_grad = expert_wgrad([(taken, 0, dgu, 0, 2 * F)], "wgrad_full")
    if fast:
        n2 = add(d2[1], after(d_far2, full_grad)[1])
        d_near2 = send("d_near2", n2, first, home3)
        dz[0] = after(dz[0], n2)
    down_grad = expert_wgrad([(dz, 0, hid, 0, F)], "wgrad_down")
    if fast:
        d_far0 = send("d_far0", d0[2:], second, d_near2)
        home2 = send("home2", total_of([d2[0], d_far2[0], d_near2]).astype(BF), links.against, down_grad)
        h1 = total_of([d1[0], d_far1[0], d_near1, home2]).astype(BF)
        home1 = send("home1", h1, links.against, got_part)
        d_near0 = send("d_near0", add(d0[1], after(d_far0, h1)[1]), first)
        m2 = add(after(done[2][0], h1), swaps[2][1, ..., :width])
        m_far2 = send("m_far2", m2[2:], second, d_far0)
        parts = [d0[0], d_far0[0], d_near0, home3, home1]
        before = (home1,)
    else:
        before = ()
    got_down = give_back(down_grad, got_part, *before)
    got_full = give_back(full_grad, got_down)

    routes_mine = lax.dynamic_slice_in_dim(routes, links.t * own_rows, own_rows, 0)
    residual_grad, branch_grad, second_gain, router_part = residual_gradient(
        parts, normed_second, residual, norm_gains[1:2], router_pad, routes_mine, cotangent
    )
    branch_group = links.gather_plane(branch_grad)
    if fast:
        m1 = add(after(done[1][0], branch_grad), swaps[1][1, ..., :width])
        m_far1 = send("m_far1", m1[2:], second, branch_grad)
        m_near2 = send("m_near2", add(m2[1], after(m_far2, branch_grad)[1]), first)
        m_home2 = send("m_home2", total_of([m2[0], m_far2[0], m_near2]).astype(BF), links.against, branch_grad)
        m3 = add(after(done[3][0], branch_grad), swaps[3][1, ..., :width])
        m_far3 = send("m_far3", m3[2:], second, branch_group)
        before = (m3, got_down)
    else:
        before = ()
    dn1, attention_grad, first_gain = attend_backward(
        heads, after(info, *before), branch_group, normed_group, attention_weights, cosine, sine, qkv, attended, lse, seqs
    )
    attention_mine = lax.psum_scatter(attention_grad, "dp", scatter_dimension=0, tiled=True).astype(F32)
    n_parts = links.scatter_plane(dn1, *([m_far3, m_far1] if fast else []))
    first_grad = total_of(n_parts)
    small = jnp.concatenate([router_part, first_gain / norm_gains[0:1], second_gain])
    small = jnp.pad(small, ((0, 6), (0, 0)))
    if fast:
        m_near1 = send("m_near1", add(m1[1], m_far1[1]), first, n_parts[1])
        m0 = add(after(done[0][0], n_parts[1]), swaps[0][1, ..., :width])
        m_far0 = send("m_far0", m0[2:], second)
        m_near3 = send("m_near3", add(m3[1], m_far3[1]), first, n_parts[1], got_full)
        m_near0 = send("m_near0", add(m0[1], m_far0[1]), first, attention_mine)
        m_home3 = send("m_home3", total_of([m3[0], m_far3[0], m_near3]).astype(BF), links.along)
        m_home1 = send("m_home1", total_of([m1[0], m_far1[0], m_near1, m_home2]).astype(BF), links.against)
        out = [m0[0], m_far0[0], m_near0, m_home1, m_home3]
        before = (m_near0, m_near3)
    else:
        out = links.scatter_group([(d[0], d[2][1, ..., :width]) for d in done])
    expert_in_grad, expert_out_grad = unpack_experts(after(got_full, *before), got_down, got_part, experts, group)
    small = links.sum_all(small, *before)
    layer_output = (residual + total_of(out)).astype(BF)

    unit = rms_unit(inputs)
    inner = first_grad * norm_gains[0]
    inverse = lax.rsqrt(jnp.mean(inputs * inputs, axis=-1, keepdims=True) + EPS)
    input_grad = residual_grad + inverse * (inner - unit * jnp.mean(inner * unit, axis=-1, keepdims=True))

    q_wide, kv_wide = heads * GRP * HD, heads * HD
    split = lambda at, size: attention_mine[:, at : at + size].reshape(depth, heads, -1)
    qkv_grad = jnp.transpose(
        jnp.concatenate(
            [split(0, q_wide), split(q_wide, kv_wide), split(q_wide + kv_wide, kv_wide)], axis=2
        ),
        (1, 0, 2),
    )
    out_weight_grad = jnp.transpose(split(q_wide + 2 * kv_wide, q_wide), (1, 2, 0))
    return (
        layer_output,
        input_grad,
        small[E : E + 2],
        jnp.transpose(small[:E]),
        qkv_grad,
        out_weight_grad,
        expert_in_grad,
        jnp.swapaxes(expert_out_grad, 1, 2),
    )


def solution(mesh):
    rows = P(("dp", "tensor"), None)
    return jax.shard_map(
        shards,
        mesh=mesh,
        in_specs=(
            rows,
            rows,
            P("dp", None),
            P("dp", None),
            P(),
            P(),
            P("tensor", "dp", None),
            P("tensor", None, "dp"),
            P("tensor", "dp", None),
            P("tensor", None, "dp"),
        ),
        out_specs=(
            rows,
            rows,
            P(),
            P(),
            P("tensor", "dp", None),
            P("tensor", None, "dp"),
            P("tensor", "dp", None),
            P("tensor", None, "dp"),
        ),
        check_vma=False,
    )
```

```python
import functools

import jax
import jax.numpy as jnp
from jax import lax
from jax.experimental import pallas as pl
from jax.experimental.pallas import tpu as pltpu
from jax.sharding import PartitionSpec as P

HD = 64
GRP = 3
F = 512
QF = F // 4
E = 40
BLK = 256
SLOT = 88
WIN_BLOCKS = 512 // BLK
EPS = 1e-05
THETA = 10000.0
NEG = -1e30
SCALE = HD ** (-0.5)
VMEM = 60 * 1024 * 1024
BF = jnp.bfloat16
COST = pl.CostEstimate(flops=10**6, bytes_accessed=10**4, transcendentals=0)
F32 = jnp.float32


def dot_nn(a, b):
    return lax.dot_general(a, b, (((1,), (0,)), ((), ())), preferred_element_type=F32)


def dot_nt(a, b):
    return lax.dot_general(a, b, (((1,), (1,)), ((), ())), preferred_element_type=F32)


def dot_tn(a, b):
    return lax.dot_general(a, b, (((0,), (0,)), ((), ())), preferred_element_type=F32)


def params(**kw):
    return pltpu.CompilerParams(vmem_limit_bytes=VMEM, **kw)


def whole(shape):
    return pl.BlockSpec(shape, lambda *a: (0,) * len(shape), pipeline_mode=pl.Buffered(1))


class Links:
    def __init__(self, group):
        self.n_dp = lax.axis_size("dp")
        self.n_t = lax.axis_size("tensor")
        self.group = group
        self.fast = self.n_dp == 8 and self.n_t == 4 and group == 8
        self.dp = lax.axis_index("dp")
        self.t = lax.axis_index("tensor")
        if self.fast:
            devices = [(d, t) for d in range(8) for t in range(4)]
            number = lambda d, t: d * 4 + t
            ring = {0: 1, 1: 3, 3: 2, 2: 0}
            self.first = [(number(d, t), number(d, t ^ (2 if d & 1 else 1))) for d, t in devices]
            self.second = [(number(d, t), number(d, t ^ (1 if d & 1 else 2))) for d, t in devices]
            self.swap = [(number(d, t), number(d ^ 1, t)) for d, t in devices]
            self.along = [(number(d, t), number(ring[d >> 1] * 2 + (d & 1), t)) for d, t in devices]
            self.against = [(b, a) for a, b in self.along]
            self.across = [(number(d, t), number(d ^ 6, t)) for d, t in devices]
            self.level = [[(number(d, t), number(d ^ (2 * k), t)) for d, t in devices] for k in range(4)]

    def send(self, label, value, perm, *later):
        value = after(value, *later)
        with jax.named_scope(label):
            return lax.ppermute(value, ("dp", "tensor"), perm)

    def plane_order(self, core):
        one = jnp.where(core == 0, 1, 2)
        return [self.t, self.t ^ one, self.t ^ (3 - one), self.t ^ 3]

    def plane_places(self):
        if not self.fast:
            return jnp.arange(self.n_t, dtype=jnp.int32)
        one = jnp.where((self.dp & 1) == 0, 1, 2)
        diff = jnp.arange(4, dtype=jnp.int32) ^ self.t
        return jnp.where(diff == one, 1, jnp.where(diff == 3 - one, 2, diff)).astype(jnp.int32)

    def gather_plane(self, block, *later):
        if not self.fast:
            return lax.all_gather(block, "tensor", axis=0)
        near = self.send("plane_near", block, self.first, *later)
        pair = jnp.stack([block, near])
        return jnp.concatenate([pair, self.send("plane_far", pair, self.second)])

    def scatter_plane(self, parts, *later):
        if not self.fast:
            rows = parts.reshape((-1,) + parts.shape[2:])
            return [lax.psum_scatter(rows, "tensor", scatter_dimension=0, tiled=True)]
        got = self.send("parts_far", parts[2:], self.second, *later)
        return [parts[0], got[0], self.send("parts_near", add(parts[1], got[1]), self.first)]

    def chunks(self):
        return self.group * self.n_t // 8

    def chunk_sources(self):
        if not self.fast:
            base = (self.dp // self.group) * self.group * self.n_t
            own = [8 * c + jnp.arange(8, dtype=jnp.int32) for c in range(self.chunks())]
            return [base + o for o in own]
        z, core = self.dp >> 1, self.dp & 1
        place = z ^ (z >> 1)
        out = []
        for c in range(4):
            back = (place + 4 - c) & 3
            source = back ^ (back >> 1)
            mine, theirs = self.plane_order(core), self.plane_order(1 - core)
            routes = [(source ^ z) * 4 + t for t in mine] + [((source ^ z) + 4) * 4 + t for t in theirs]
            out.append(jnp.stack(routes).astype(jnp.int32))
        return out

    def groups(self):
        n = self.n_dp // self.group
        return [list(range(g * self.group, (g + 1) * self.group)) for g in range(n)]

    def gather_group(self, block):
        if self.n_dp == self.group:
            return lax.all_gather(block, ("dp", "tensor"), axis=0)
        plane = lax.all_gather(block, "tensor", axis=0)
        return lax.all_gather(plane, "dp", axis=0, axis_index_groups=self.groups()).reshape((-1,) + block.shape)

    def scatter_group(self, pairs):
        rows = jnp.concatenate([half for pair in pairs for half in pair])
        rows = rows.reshape((self.group, -1) + rows.shape[2:])
        total = lax.psum_scatter(rows, "dp", scatter_dimension=0, axis_index_groups=self.groups())
        return [lax.psum_scatter(total, "tensor", scatter_dimension=0, tiled=True)]

    def sum_all(self, value, *later):
        if not self.fast:
            return lax.psum(value, ("dp", "tensor"))
        for perm in (self.swap, self.first, self.second):
            value = value + self.send("small", value, perm)
        value = after(value, *later)
        for perm in self.level[1:3]:
            value = value + self.send("small", value, perm)
        return value


def after(value, *earlier):
    return lax.optimization_barrier((value,) + earlier)[0] if earlier else value


def total_of(parts):
    total = parts[0].astype(F32)
    for part in parts[1:]:
        total = total + part.astype(F32)
    return total


def add(a, b):
    return (a.astype(F32) + b.astype(F32)).astype(a.dtype)


def pack_attention_kernel(heads, qkv_ref, out_ref, packed_ref):
    q_wide, kv_wide = heads * GRP * HD, heads * HD
    for h in range(heads):
        one = qkv_ref[h]
        packed_ref[:, h * GRP * HD : (h + 1) * GRP * HD] = one[:, : GRP * HD]
        packed_ref[:, q_wide + h * HD : q_wide + (h + 1) * HD] = one[:, GRP * HD : (GRP + 1) * HD]
        at = q_wide + kv_wide + h * HD
        packed_ref[:, at : at + HD] = one[:, (GRP + 1) * HD :]
        at = q_wide + 2 * kv_wide + h * GRP * HD
        packed_ref[:, at : at + GRP * HD] = out_ref[h].astype(F32).T.astype(BF)


def pack_attention(qkv_weight, out_weight):
    heads, depth, _ = qkv_weight.shape
    return pl.pallas_call(
        functools.partial(pack_attention_kernel, heads),
        out_shape=jax.ShapeDtypeStruct((depth, heads * (2 * GRP + 2) * HD), BF),
        compiler_params=params(),
        name="pack_attention",
    )(qkv_weight, out_weight)


def attention_places(links):
    if not links.fast:
        return jnp.arange(links.n_dp, dtype=jnp.int32)
    z, core = links.dp >> 1, links.dp & 1
    near = [(z ^ k) * 2 for k in range(4)]
    return jnp.stack([n + core for n in near] + [n + 1 - core for n in near]).astype(jnp.int32)


def pack_kernel(gate_ref, up_ref, part_ref, down_ref, packed_ref):
    packed_ref[0, :, :QF] = gate_ref[0]
    packed_ref[0, :, QF : 2 * QF] = up_ref[0]
    packed_ref[0, :, 2 * QF : 3 * QF] = part_ref[0]
    packed_ref[0, :, 3 * QF :] = down_ref[0]


def pack_experts(expert_in, expert_out_t, group, n_dp):
    depth = expert_in.shape[1]
    of = lambda d: d % group
    return pl.pallas_call(
        pack_kernel,
        grid=(n_dp,),
        in_specs=[
            pl.BlockSpec((1, depth, QF), lambda d: (group + of(d) // 4, 0, of(d) % 4)),
            pl.BlockSpec((1, depth, QF), lambda d: (group + of(d) // 4, 0, 4 + of(d) % 4)),
            pl.BlockSpec((1, depth, QF), lambda d: (group + of(d) // 4, 0, of(d) % 4)),
            pl.BlockSpec((1, depth, F), lambda d: (of(d), 0, 0)),
        ],
        out_specs=pl.BlockSpec((1, depth, 3 * QF + F), lambda d: (d, 0, 0)),
        out_shape=jax.ShapeDtypeStruct((n_dp, depth, 3 * QF + F), BF),
        compiler_params=params(),
        name="pack_experts",
    )(expert_in, expert_in, expert_out_t, expert_out_t)


def unpack_kernel(group, full_ref, down_ref, part_ref, in_ref, out_ref):
    e = pl.program_id(0)

    @pl.when(e < group)
    def _():
        in_ref[0] = full_ref[0].astype(F32)
        out_ref[0] = down_ref[0].astype(F32)

    @pl.when(e >= group)
    def _():
        for q in range(4):
            part = part_ref[(e - group) * 4 + q].astype(F32)
            in_ref[0, :, q * QF : (q + 1) * QF] = part[:, :QF]
            in_ref[0, :, F + q * QF : F + (q + 1) * QF] = part[:, QF : 2 * QF]
            out_ref[0, :, q * QF : (q + 1) * QF] = part[:, 2 * QF :]


def unpack_experts(full, down, part, experts, group):
    depth = full.shape[1]
    first = lambda e: (jnp.minimum(e, group - 1), 0, 0)
    return pl.pallas_call(
        functools.partial(unpack_kernel, group),
        grid=(experts,),
        in_specs=[
            pl.BlockSpec((1, depth, 2 * F), first),
            pl.BlockSpec((1, depth, F), first),
            whole(part.shape),
        ],
        out_specs=(
            pl.BlockSpec((1, depth, 2 * F), lambda e: (e, 0, 0)),
            pl.BlockSpec((1, depth, F), lambda e: (e, 0, 0)),
        ),
        out_shape=(
            jax.ShapeDtypeStruct((experts, depth, 2 * F), F32),
            jax.ShapeDtypeStruct((experts, depth, F), F32),
        ),
        compiler_params=params(),
        name="unpack_experts",
    )(full, down, part)


def expert_kernel(
    info_ref, xa_ref, xb_ref, ya_ref, yb_ref, routes_ref, router_ref, full_ref, rest_ref,
    ma_ref, da_ref, theirs_ref, taken_ref, dz_ref, dgu_ref, hid_ref,
):
    step = pl.program_id(0)
    first, second = info_ref[0], info_ref[1]
    expert_id = lax.broadcasted_iota(jnp.int32, (E, BLK), 0)
    slot_id = lax.broadcasted_iota(jnp.int32, (SLOT, BLK), 0)
    upto = (
        lax.broadcasted_iota(jnp.int32, (BLK, BLK), 0) <= lax.broadcasted_iota(jnp.int32, (BLK, BLK), 1)
    ).astype(BF)
    row_id = lax.broadcasted_iota(jnp.int32, (8, BLK), 0)
    picks, slot_gates, taken, dz = [], ([], []), ([], []), ([], [])
    for b in range(4):
        x = (xa_ref if b < 2 else xb_ref)[b % 2].reshape(BLK, -1)
        y = (ya_ref if b < 2 else yb_ref)[b % 2].reshape(BLK, -1)
        routes = routes_ref[info_ref[2 + step * 2 + b % 2 + (0 if b < 2 else 4)]]
        logits = dot_nt(router_ref[...], x)
        member = expert_id == routes[0:1]
        for k in range(1, 8):
            member = member | (expert_id == routes[k : k + 1])
        masked = jnp.where(member, logits, NEG)
        shifted = jnp.exp(masked - jnp.max(masked, axis=0, keepdims=True))
        shifted = jnp.where(member, shifted, 0.0)
        gates = shifted / jnp.sum(shifted, axis=0, keepdims=True)
        member = member.astype(F32)
        rows = []
        for e in (first, second):
            here = expert_id == e
            rows.append(
                (
                    jnp.sum(jnp.where(here, gates, 0.0), axis=0, keepdims=True),
                    jnp.sum(jnp.where(here, member, 0.0), axis=0, keepdims=True),
                )
            )
        both = jnp.where(row_id == 0, rows[0][1], jnp.where(row_id == 1, rows[1][1], 0.0))
        counts = dot_nn(both.astype(BF), upto).astype(jnp.int32)
        pick = []
        for j in range(2):
            spot = jnp.where(rows[j][1] > 0.0, counts[j : j + 1] - 1, -1)
            hot = (slot_id == spot).astype(F32)
            slot_gates[j].append(jnp.sum(hot * rows[j][0], axis=1, keepdims=True))
            pick.append(hot)
        pick = jnp.concatenate(pick, axis=0).astype(BF)
        picks.append(pick)
        got = dot_nn(pick, x)
        taken[0].append(got[:SLOT])
        taken[1].append(got[SLOT:])
        got = dot_nn(pick, y)
        dz[0].append(got[:SLOT])
        dz[1].append(got[SLOT:])
    sends, backs = [], []
    for j in range(2):
        width = F if j == 0 else QF
        in_at = 0 if j == 0 else 2 * F
        rows = jnp.concatenate(taken[j], axis=0).astype(BF)
        grads = jnp.concatenate(dz[j], axis=0).astype(BF)
        gate = jnp.concatenate(slot_gates[j], axis=0)
        taken_ref[0, j] = rows
        dz_ref[0, j] = grads
        w_in = full_ref[...] if j == 0 else rest_ref[:, : 2 * QF]
        w_out = rest_ref[:, 3 * QF :] if j == 0 else rest_ref[:, 2 * QF : 3 * QF]
        gate_up = dot_nn(rows, w_in)
        gate_part, up_part = gate_up[:, :width], gate_up[:, width:]
        sig = 1.0 / (1.0 + jnp.exp(-gate_part))
        silu = gate_part * sig
        hidden = silu * up_part
        scaled = (gate * hidden).astype(BF)
        hid_at = 0 if j == 0 else F
        hid_ref[0, :, hid_at : hid_at + width] = scaled
        sends.append(dot_nt(scaled, w_out))
        raw = dot_nn(grads, w_out)
        dgate = jnp.sum(hidden.astype(BF).astype(F32) * raw, axis=1, keepdims=True)
        dhid = gate * raw
        dgu = jnp.concatenate(
            [dhid * up_part * (sig * (1.0 + gate_part * (1.0 - sig))), dhid * silu], axis=1
        ).astype(BF)
        dgu_ref[0, :, in_at : in_at + 2 * width] = dgu
        back = dot_nt(dgu, w_in)
        lane = lax.broadcasted_iota(jnp.int32, (1, 128), 1)
        e = first if j == 0 else second
        high = dgate.astype(BF).astype(F32)
        extra = jnp.where(lane == e, high, 0.0) + jnp.where(lane == e + 64, dgate - high, 0.0)
        backs.append(jnp.concatenate([back, extra], axis=1))
    for b in range(4):
        at = slice(b * SLOT, (b + 1) * SLOT)
        for kind, values in enumerate((backs, sends)):
            stacked = jnp.concatenate([values[0][at], values[1][at]], axis=0).astype(BF)
            summed = dot_tn(picks[b], stacked).astype(BF)
            if b < 2:
                (da_ref, ma_ref)[kind][b] = summed
            else:
                theirs_ref[kind, b - 2, :, : summed.shape[1]] = summed


def stepped(shape):
    return pl.BlockSpec((1,) + shape[1:], lambda s, *_: (s,) + (0,) * (len(shape) - 1))


def expert_chunk(info, rows, routes, router_t, weights):
    width = rows[0][0].shape[-1]
    shape = jax.ShapeDtypeStruct
    half = pl.BlockSpec((2, BLK, width), lambda s, i: (s, 0, 0))

    def given(array, column):
        if column is None:
            return half
        return pl.BlockSpec((2, 1, BLK, width), lambda s, i: (s, column, 0, 0))

    slots = 4 * SLOT
    kept = [
        shape((2, 2, slots, width), BF),
        shape((2, 2, slots, width), BF),
        shape((2, slots, 2 * F + 2 * QF), BF),
        shape((2, slots, F + QF), BF),
    ]
    return pl.pallas_call(
        expert_kernel,
        grid_spec=pltpu.PrefetchScalarGridSpec(
            num_scalar_prefetch=1,
            grid=(2,),
            in_specs=[given(*r) for r in rows] + [whole(a.shape) for a in (routes, router_t, *weights)],
            out_specs=[
                half,
                pl.BlockSpec((2, BLK, width + 128), lambda s, i: (s, 0, 0)),
                pl.BlockSpec((2, 2, BLK, width + 128), lambda s, i: (0, s, 0, 0)),
            ]
            + [stepped(s.shape) for s in kept],
        ),
        out_shape=[
            shape((4, BLK, width), BF),
            shape((4, BLK, width + 128), BF),
            shape((2, 4, BLK, width + 128), BF),
        ]
        + kept,
        compiler_params=params(),
        cost_estimate=pl.CostEstimate(flops=30 * 10**9, bytes_accessed=45 * 10**6, transcendentals=10**6),
        name="experts",
    )(info, *[r[0] for r in rows], routes, router_t, *weights)


def wgrad_kernel(chunks, pairs, *refs):
    out_ref = refs[-1]
    flat = lambda v: v.reshape((-1, v.shape[-1]))
    at = 0
    for p in range(pairs):
        left, right = refs[2 * p * chunks : (2 * p + 1) * chunks], refs[(2 * p + 1) * chunks : (2 * p + 2) * chunks]
        total = dot_tn(flat(left[0][...]), flat(right[0][...]))
        for l, r in zip(left[1:], right[1:]):
            total = total + dot_tn(flat(l[...]), flat(r[...]))
        out_ref[:, at : at + total.shape[1]] = total.astype(BF)
        at += total.shape[1]


def expert_wgrad(pairs, name):
    width = pairs[0][0][0].shape[-1]
    chunks = len(pairs[0][0])
    tile = 256
    specs, operands, columns = [], [], 0
    for left, j, right, at, size in pairs:
        rows = left[0].shape[2]
        specs += [pl.BlockSpec((2, 1, rows, tile), lambda k, j=j: (0, j, 0, k))] * chunks
        specs += [
            pl.BlockSpec((2, rows, size), lambda k, b=at // size: (0, 0, b), pipeline_mode=pl.Buffered(1))
        ] * chunks
        operands += list(left) + list(right)
        columns += size
    return pl.pallas_call(
        functools.partial(wgrad_kernel, chunks, len(pairs)),
        grid=(width // tile,),
        in_specs=specs,
        out_specs=pl.BlockSpec((tile, columns), lambda k: (k, 0)),
        out_shape=jax.ShapeDtypeStruct((width, columns), BF),
        compiler_params=params(),
        cost_estimate=COST,
        name=name,
    )(*operands)


def swap_halves(values):
    width = values.shape[1]
    lane = lax.broadcasted_iota(jnp.int32, values.shape, 1)
    up = pltpu.roll(values, width - HD // 2, 1)
    down = pltpu.roll(values, HD // 2, 1)
    return jnp.where((lane & (HD - 1)) < HD // 2, up, down)


def spread(table, width):
    return jnp.concatenate([table] * (width // 128), axis=1)


def allowed_mask(starts, block, window):
    first = (block - window + 1) * BLK
    shape = (BLK, window * BLK)
    query = block * BLK + lax.broadcasted_iota(jnp.int32, shape, 0)
    key = first + lax.broadcasted_iota(jnp.int32, shape, 1)
    begin = jnp.zeros(shape, jnp.int32)
    for s in starts:
        begin = jnp.where(query >= s, s, begin)
    return (key >= begin) & (key <= query)


def over_windows(block, blocks, body):
    for w in range(1, min(WIN_BLOCKS + 1, blocks) + 1):
        last = w == WIN_BLOCKS + 1
        pl.when((block >= w - 1) if last else (block == w - 1))(functools.partial(body, w))


def heads_to_rows(values, first):
    return jnp.concatenate([values[:, (first + g) * HD : (first + g + 1) * HD] for g in range(GRP)], axis=0)


def rows_to_heads(values):
    return [values[g * BLK : (g + 1) * BLK] for g in range(GRP)]


def attend_kernel(heads, blocks, seqs, pieces, info_ref, n1_ref, cos_ref, sin_ref, *refs):
    out_ref, qkv_ref, o_ref, lse_ref, w_ref = refs[pieces:]
    i = pl.program_id(0)

    @pl.when(i == 0)
    def _():
        each = [ref.at[p] for ref in refs[:pieces] for p in range(ref.shape[0])]
        depth = w_ref.shape[0] // len(each)
        for k, piece in enumerate(each):
            at = pl.multiple_of(info_ref[blocks + seqs + k] * depth, depth)
            w_ref[pl.ds(at, depth), :] = piece[:depth]

    q_wide, kv_wide = heads * GRP * HD, heads * HD
    rot_wide, qkv_wide = q_wide + kv_wide, q_wide + 2 * kv_wide
    projected = dot_nn(n1_ref[0], w_ref[:, :qkv_wide])
    turning = projected[:, :rot_wide]
    turned = turning * spread(cos_ref[...], rot_wide) + swap_halves(turning) * spread(sin_ref[...], rot_wide)
    rows = pl.ds(pl.multiple_of(i * BLK, BLK), BLK)
    queries = (turned[:, :q_wide].astype(BF).astype(F32) * SCALE).astype(BF)
    qkv_ref[rows, :q_wide] = queries
    qkv_ref[rows, q_wide:rot_wide] = turned[:, q_wide:].astype(BF)
    qkv_ref[rows, rot_wide:] = projected[:, rot_wide:].astype(BF)
    starts = [info_ref[blocks + s] for s in range(seqs)]

    def attend(window):
        keep = allowed_mask(starts, i, window)
        keys = pl.ds(pl.multiple_of((i - window + 1) * BLK, BLK), window * BLK)
        lane = lax.broadcasted_iota(jnp.int32, (BLK, 128), 1)
        lse_all = jnp.zeros((BLK, 128), F32)
        attended = []
        for h in range(heads):
            k_rows = qkv_ref[keys, q_wide + h * HD : q_wide + (h + 1) * HD]
            v_rows = qkv_ref[keys, rot_wide + h * HD : rot_wide + (h + 1) * HD]
            scores = dot_nt(heads_to_rows(queries, h * GRP), k_rows)
            for g in range(GRP):
                part = jnp.where(keep, scores[g * BLK : (g + 1) * BLK], NEG)
                top = jnp.max(part, axis=1, keepdims=True)
                shifted = jnp.exp(part - top)
                total = jnp.sum(shifted, axis=1, keepdims=True)
                probability = (shifted * (1.0 / total)).astype(BF)
                attended.append(dot_nn(probability, v_rows).astype(BF))
                lse_all = jnp.where(lane == h * GRP + g, top + jnp.log(total), lse_all)
        lse_ref[...] = lse_all
        attended = jnp.concatenate(attended, axis=1)
        o_ref[...] = attended
        out_ref[0] = dot_nt(attended, w_ref[:, qkv_wide:]).astype(BF)

    over_windows(i, blocks, attend)


def attend_forward(heads, info, normed, pieces, cosine, sine, seqs):
    blocks, _, width = normed.shape
    rows = blocks * BLK
    q_wide = heads * GRP * HD
    qkv_wide = q_wide + 2 * heads * HD
    shape = jax.ShapeDtypeStruct
    weights = (width, pieces[0].shape[-1])
    return pl.pallas_call(
        functools.partial(attend_kernel, heads, blocks, seqs, len(pieces)),
        grid_spec=pltpu.PrefetchScalarGridSpec(
            num_scalar_prefetch=1,
            grid=(blocks,),
            in_specs=[
                pl.BlockSpec((1, BLK, width), lambda i, info: (info[i], 0, 0)),
                pl.BlockSpec((BLK, 128), lambda i, info: (i, 0)),
                pl.BlockSpec((BLK, 128), lambda i, info: (i, 0)),
            ]
            + [whole(p.shape) for p in pieces],
            out_specs=[
                pl.BlockSpec((1, BLK, width), lambda i, info: (info[i], 0, 0)),
                whole((rows, qkv_wide)),
                pl.BlockSpec((BLK, q_wide), lambda i, info: (i, 0)),
                pl.BlockSpec((BLK, 128), lambda i, info: (i, 0)),
                whole(weights),
            ],
        ),
        out_shape=[
            shape((blocks, BLK, width), BF),
            shape((rows, qkv_wide), BF),
            shape((rows, q_wide), BF),
            shape((rows, 128), F32),
            shape(weights, BF),
        ],
        compiler_params=params(),
        cost_estimate=COST,
        name="attend",
    )(info, normed, cosine, sine, *pieces)


def attend_back_kernel(
    heads,
    blocks,
    seqs,
    info_ref,
    da_ref,
    n1_ref,
    w_ref,
    cos_ref,
    sin_ref,
    qkv_ref,
    o_ref,
    lse_ref,
    dn1_ref,
    dw_ref,
    gain_ref,
    acc_ref,
    dq_ref,
    dkv_ref,
):
    step = pl.program_id(0)
    q_wide, kv_wide = heads * GRP * HD, heads * HD
    rot_wide, qkv_wide = q_wide + kv_wide, q_wide + 2 * kv_wide
    starts = [info_ref[blocks + s] for s in range(seqs)]

    @pl.when(step == 0)
    def _():
        acc_ref[...] = jnp.zeros_like(acc_ref)
        dkv_ref[...] = jnp.zeros_like(dkv_ref)
        gain_ref[...] = jnp.zeros_like(gain_ref)

    @pl.when(step < blocks)
    def _():
        i = step
        da = da_ref[0]
        w_out = w_ref[:, qkv_wide:]
        grad = dot_nn(da, w_out).astype(BF)
        acc_ref[:, qkv_wide:] += dot_tn(da, o_ref[...])
        rows = pl.ds(pl.multiple_of(i * BLK, BLK), BLK)
        queries = qkv_ref[rows, :q_wide]
        lse = lse_ref[...]

        def back(window):
            keep = allowed_mask(starts, i, window)
            keys = pl.ds(pl.multiple_of((i - window + 1) * BLK, BLK), window * BLK)
            for h in range(heads):
                k_rows = qkv_ref[keys, q_wide + h * HD : q_wide + (h + 1) * HD]
                v_rows = qkv_ref[keys, rot_wide + h * HD : rot_wide + (h + 1) * HD]
                stacked_q = heads_to_rows(queries, h * GRP)
                stacked_g = heads_to_rows(grad, h * GRP)
                scores = dot_nt(stacked_q, k_rows)
                dprob = dot_nt(stacked_g, v_rows)
                probs, dscores = [], []
                for g in range(GRP):
                    at = slice(g * BLK, (g + 1) * BLK)
                    one = h * GRP + g
                    prob = jnp.where(keep, jnp.exp(scores[at] - lse[:, one : one + 1]), 0.0)
                    both = prob * dprob[at]
                    inner = jnp.sum(both, axis=1, keepdims=True)
                    dscores.append((both - prob * inner).astype(BF))
                    probs.append(prob.astype(BF))
                probs = jnp.concatenate(probs, axis=0)
                dscores = jnp.concatenate(dscores, axis=0)
                dq = dot_nn(dscores, k_rows) * SCALE
                dq_ref[rows, h * GRP * HD : (h + 1) * GRP * HD] = jnp.concatenate(rows_to_heads(dq), axis=1)
                dkv_ref[h, keys, :HD] += dot_tn(dscores, stacked_q)
                dkv_ref[h, keys, HD:] += dot_tn(probs, stacked_g)

        over_windows(i, blocks, back)

    @pl.when(step >= blocks)
    def _():
        j = step - blocks
        rows = pl.ds(pl.multiple_of(j * BLK, BLK), BLK)
        dk = [dkv_ref[h, rows, :HD] for h in range(heads)]
        dv = [dkv_ref[h, rows, HD:] for h in range(heads)]
        turned = jnp.concatenate([dq_ref[rows, :]] + dk, axis=1)
        turned = turned * spread(cos_ref[...], rot_wide) - swap_halves(turned) * spread(sin_ref[...], rot_wide)
        dqkv = jnp.concatenate([turned] + dv, axis=1).astype(BF)
        n1 = n1_ref[0]
        acc_ref[:, :qkv_wide] += dot_tn(n1, dqkv)
        dn1 = dot_nt(dqkv, w_ref[:, :qkv_wide])
        gain_ref[...] += jnp.sum(dn1 * n1.astype(F32), axis=0, keepdims=True)
        dn1_ref[0] = dn1.astype(BF)

    @pl.when(step == 2 * blocks - 1)
    def _():
        dw_ref[...] = acc_ref[...].astype(BF)


def attend_backward(heads, info, da, normed, weights, cosine, sine, qkv, attended, lse, seqs):
    blocks, _, width = normed.shape
    rows = blocks * BLK
    q_wide = heads * GRP * HD
    shape = jax.ShapeDtypeStruct
    early = lambda i: jnp.minimum(i, blocks - 1)
    late = lambda i: jnp.maximum(i - blocks, 0)
    return pl.pallas_call(
        functools.partial(attend_back_kernel, heads, blocks, seqs),
        grid_spec=pltpu.PrefetchScalarGridSpec(
            num_scalar_prefetch=1,
            grid=(2 * blocks,),
            in_specs=[
                pl.BlockSpec((1, BLK, width), lambda i, info: (info[early(i)], 0, 0)),
                pl.BlockSpec((1, BLK, width), lambda i, info: (info[late(i)], 0, 0)),
                whole(weights.shape),
                pl.BlockSpec((BLK, 128), lambda i, info: (late(i), 0)),
                pl.BlockSpec((BLK, 128), lambda i, info: (late(i), 0)),
                whole(qkv.shape),
                pl.BlockSpec((BLK, q_wide), lambda i, info: (early(i), 0)),
                pl.BlockSpec((BLK, 128), lambda i, info: (early(i), 0)),
            ],
            out_specs=[
                pl.BlockSpec((1, BLK, width), lambda i, info: (info[late(i)], 0, 0)),
                whole(weights.shape),
                whole((1, width)),
            ],
            scratch_shapes=[
                pltpu.VMEM(weights.shape, F32),
                pltpu.VMEM((rows, q_wide), F32),
                pltpu.VMEM((heads, rows, 2 * HD), F32),
            ],
        ),
        out_shape=[shape((blocks, BLK, width), BF), shape(weights.shape, BF), shape((1, width), F32)],
        compiler_params=params(),
        cost_estimate=COST,
        name="attend_back",
    )(info, da, normed, weights, cosine, sine, qkv, attended, lse)


def residual_kernel(parts, *refs):
    part_refs = refs[:parts]
    n2_ref, h_ref, gain_ref, router_ref, routes_ref, cot_ref, dh_ref, da_ref, dgain_ref, drouter_ref = refs[parts:]
    width = n2_ref.shape[1]
    total = total_of([r[...] for r in part_refs])
    dn2 = total[:, :width]
    dgate = total[:, width:]
    dgate = dgate + pltpu.roll(dgate, 64, 1)
    n2 = n2_ref[...]
    logits = dot_nt(n2, router_ref[...])
    lane = lax.broadcasted_iota(jnp.int32, logits.shape, 1)
    routes = routes_ref[...]
    member = lane == routes[:, 0:1]
    for k in range(1, 8):
        member = member | (lane == routes[:, k : k + 1])
    masked = jnp.where(member, logits, NEG)
    shifted = jnp.where(member, jnp.exp(masked - jnp.max(masked, axis=1, keepdims=True)), 0.0)
    gates = shifted / jnp.sum(shifted, axis=1, keepdims=True)
    dgate = jnp.where(member, dgate, 0.0)
    dlogit = gates * (dgate - jnp.sum(gates * dgate, axis=1, keepdims=True))
    high = dlogit.astype(BF)
    low = (dlogit - high.astype(F32)).astype(BF)
    dn2 = dn2 + dot_nn(high, router_ref[...]) + dot_nn(low, router_ref[...])
    drouter_ref[...] = (dot_tn(high, n2) + dot_tn(low, n2))[:E]
    h = h_ref[...]
    inverse = lax.rsqrt(jnp.mean(h * h, axis=1, keepdims=True) + EPS)
    unit = h * inverse
    dgain_ref[...] = jnp.sum(dn2 * unit, axis=0, keepdims=True)
    inner = dn2 * gain_ref[...]
    dh = cot_ref[...].astype(F32) + inverse * (inner - unit * jnp.mean(inner * unit, axis=1, keepdims=True))
    dh_ref[...] = dh
    da_ref[...] = dh.astype(BF)


def residual_gradient(parts, n2, h, gain, router_pad, routes, cotangent):
    rows, width = n2.shape
    shape = jax.ShapeDtypeStruct
    return pl.pallas_call(
        functools.partial(residual_kernel, len(parts)),
        out_shape=[
            shape((rows, width), F32),
            shape((rows, width), BF),
            shape((1, width), F32),
            shape((E, width), F32),
        ],
        compiler_params=params(),
        cost_estimate=COST,
        name="residual_gradient",
    )(*parts, n2, h, gain, router_pad, routes, cotangent)


def rms_unit(values):
    return values * lax.rsqrt(jnp.mean(values * values, axis=-1, keepdims=True) + EPS)


def rope_tables(starts, rows):
    index = jnp.arange(rows, dtype=jnp.int32)
    begin = jnp.max(jnp.where(index[:, None] >= starts[None, :], starts[None, :], 0), axis=1)
    position = (index - begin).astype(F32)
    halfway = HD // 2
    frequency = THETA ** (-(jnp.arange(halfway, dtype=F32) * 2.0 / HD))
    angles = position[:, None] * frequency[None, :]
    cosine, sine = jnp.cos(angles), jnp.sin(angles)
    return (
        jnp.concatenate([cosine] * 4, axis=1),
        jnp.concatenate([-sine, sine, -sine, sine], axis=1),
    )


def shards(tokens, cotangent, lengths, routes, norm_gains, router_weight, qkv_weight, out_weight, expert_in, expert_out):
    own_rows, width = tokens.shape
    group_rows = routes.shape[0]
    heads = qkv_weight.shape[0]
    experts, depth, _ = expert_in.shape
    group = experts * 4 // 5
    n_dp = lax.axis_size("dp")
    links = Links(group)
    fast = links.fast
    send, first, second = links.send, (links.first if fast else None), (links.second if fast else None)
    rank = links.dp % group
    own_expert = links.t * experts + rank
    part_expert = links.t * experts + group + rank // 4
    seqs = lengths.shape[1]
    blocks = group_rows // own_rows
    inputs = tokens.astype(F32)
    expert_out_t = jnp.swapaxes(expert_out, 1, 2)
    starts = jnp.cumsum(lengths[0]) - lengths[0]
    cosine, sine = rope_tables(starts, group_rows)
    info = jnp.concatenate([links.plane_places(), starts.astype(jnp.int32), attention_places(links)])
    router_t = jnp.transpose(router_weight)
    router_pad = jnp.pad(router_t, ((0, 128 - E), (0, 0)))
    mine = jnp.stack([own_expert, part_expert]).astype(jnp.int32)
    sources = links.chunk_sources()
    chunks = links.chunks()
    to_all = lambda a: lax.all_to_all(a, "dp", 0, 0)

    shard = pack_attention(qkv_weight, out_weight)
    normed_first = (rms_unit(inputs) * norm_gains[0]).astype(BF)
    packed = pack_experts(expert_in, expert_out_t, group, n_dp)
    own_in = expert_in[:group] if n_dp == group else jnp.concatenate([expert_in[:group]] * (n_dp // group))
    routes_t = jnp.transpose(routes)
    by_block = lambda r: jnp.transpose(r.reshape(-1, 8, blocks, own_rows), (0, 2, 1, 3)).reshape(-1, 8, own_rows)
    if fast:
        y, swap = cotangent, links.swap
        routes_rows = jnp.pad(routes_t.astype(BF), ((0, 8), (0, 0)))
        shard = jnp.concatenate([shard, routes_rows])
        pieces = [send("pieces", shard, links.level[k]) for k in range(1, 4)]
        near = send("near", normed_first, first, shard)
        pair = jnp.stack([normed_first, near])
        far = send("far", pair, second)

        pieces_mine = jnp.stack([shard] + pieces)
        pieces_theirs = send("pieces_theirs", pieces_mine, swap)
        y_near0 = send("y_near0", y, first, far)
        rest = to_all(after(packed, pieces_mine))
        normed_group = jnp.concatenate([pair, far])
        y_pair0 = jnp.stack([y, y_near0])
        y_far0 = send("y_far0", y_pair0, second)
        attend_pieces = [pieces_mine, pieces_theirs]
        routes_all = jnp.concatenate([pieces_mine[:, depth : depth + 8], pieces_theirs[:, depth : depth + 8]])
        routes_all = by_block(routes_all).astype(jnp.int32)
        before = (rest, y_far0)
    else:
        normed_group = links.gather_plane(normed_first)
        attend_pieces = [lax.all_gather(shard, "dp", axis=0)]
        rest = to_all(packed)
        routes_all = by_block(lax.all_gather(routes_t, "dp", axis=0))
        before = (packed,)
    mixed, qkv, attended, lse, attention_weights = attend_forward(
        heads, after(info, *before), normed_group, attend_pieces, cosine, sine, seqs
    )
    if fast:
        full = to_all(after(own_in, rest))
        h_far = send("h_far", mixed[2:], second)
        h_near = send("h_near", add(mixed[1], h_far[1]), first)
        y_mine0 = jnp.concatenate([y_pair0, after(y_far0, mixed)])
        y_theirs0 = send("y_theirs0", y_mine0, swap)
        residual = inputs + total_of([mixed[0], h_far[0], h_near])
    else:
        full = to_all(own_in)
        residual = inputs + total_of(links.scatter_plane(mixed))
    weights = [w.reshape(width, -1) for w in (full, rest)]
    normed_second = (rms_unit(residual) * norm_gains[1]).astype(BF)
    x = after(normed_second, full)

    def run(c, rows, *later):
        chunk_info = after(jnp.concatenate([mine, sources[c]]), *later)
        return expert_chunk(chunk_info, rows, routes_all, router_t, weights)

    if fast:
        both = jnp.stack([x, y])
        near0 = send("near0", x, first, both)
        both1 = send("both1", both, links.along)
        both3 = send("both3", both, links.against)
        pair0 = jnp.stack([x, near0])
        far0 = send("far0", pair0, second)
        mine0 = jnp.concatenate([pair0, far0])
        near1 = send("near1", both1, first)
        theirs0 = send("theirs0", mine0, swap, y_theirs0, near1)
        both2 = send("both2", both1, links.along)
        pair1 = jnp.stack([both1, near1])
        far1 = send("far1", pair1, second)
        done0 = run(0, [(mine0, None), (theirs0, None), (y_mine0, None), (y_theirs0, None)], pair1)
        past = done0[-1]
        near3 = send("near3", both3, first, past)
        mine1 = jnp.concatenate([after(pair1, past), after(far1, past)])
        theirs1 = send("theirs1", mine1, swap, both3)
        swap0 = send("swap0", done0[2], swap, mine1)
        pair3 = jnp.stack([after(both3, past), after(near3, past)])
        far3 = send("far3", pair3, second)

        done1 = run(1, [(mine1, 0), (theirs1, 0), (mine1, 1), (theirs1, 1)], pair3)
        past = done1[-1]
        near2 = send("near2", both2, first, past)
        mine3 = jnp.concatenate([after(pair3, past), after(far3, past)])
        pair2 = jnp.stack([after(both2, past), after(near2, past)])
        theirs3 = send("theirs3", mine3, swap, both2)
        far2 = send("far2", pair2, second)
        swap1 = send("swap1", done1[2], swap, mine3)
        d0 = add(after(done0[1], pair2), after(swap0, past)[0])
        done3 = run(3, [(mine3, 0), (theirs3, 0), (mine3, 1), (theirs3, 1)], pair2, d0)
        past = done3[-1]
        mine2 = jnp.concatenate([after(pair2, past), after(far2, past)])
        theirs2 = send("theirs2", mine2, swap)
        swap3 = send("swap3", done3[2], swap, mine2)
        d1 = add(after(done1[1], mine2), after(swap1, past)[0])
        d_far1 = send("d_far1", d1[2:], second)
        d3 = add(after(done3[1], d1), swap3[0])
        d_far3 = send("d_far3", d3[2:], second)
        done2 = run(2, [(mine2, 0), (theirs2, 0), (mine2, 1), (theirs2, 1)], d3)
        past = done2[-1]
        done = [done0, done1, done2, done3]
    else:
        x_all, y_all = links.gather_group(x), links.gather_group(cotangent)
        halves = lambda a, c: [(a[8 * c : 8 * c + 4], None), (a[8 * c + 4 : 8 * c + 8], None)]
        done = [run(c, halves(x_all, c) + halves(y_all, c)) for c in range(chunks)]
        parts = links.scatter_group([(d[1], d[2][0]) for d in done])
    taken, dz, dgu, hid = ([d[k] for d in done] for k in range(3, 7))
    if fast:
        swap2 = send("swap2", done2[2], swap, d_far1, d_far3)
        swaps = [swap0, swap1, swap2, swap3]
        n1, n3 = add(d1[1], d_far1[1]), add(d3[1], after(d_far3, past)[1])
        d_near3 = send("d_near3", n3, first)
        d_near1 = send("d_near1", n1, first, past)
        hid[0] = after(hid[0], n1, n3)
    part_grad = expert_wgrad([(taken, 1, dgu, 2 * F, 2 * QF), (dz, 1, hid, F, QF)], "wgrad_part")

    def give_back(grad, *later):
        got = to_all(after(grad.reshape(n_dp, depth, -1), *later))
        if n_dp == group:
            return got
        return jnp.sum(got.reshape((-1, group) + got.shape[1:]).astype(F32), axis=0).astype(BF)

    if fast:
        d2 = add(after(done2[1], part_grad), swap2[0])
        d_far2 = send("d_far2", d2[2:], second)
        home3 = send("home3", total_of([d3[0], d_far3[0], d_near3]).astype(BF), links.along, part_grad)
        taken[0] = after(taken[0], d2)
    got_part = give_back(part_grad)
    full_grad = expert_wgrad([(taken, 0, dgu, 0, 2 * F)], "wgrad_full")
    if fast:
        n2 = add(d2[1], after(d_far2, full_grad)[1])
        d_near2 = send("d_near2", n2, first, home3)
        dz[0] = after(dz[0], n2)
    down_grad = expert_wgrad([(dz, 0, hid, 0, F)], "wgrad_down")
    if fast:
        d_far0 = send("d_far0", d0[2:], second, d_near2)
        home2 = send("home2", total_of([d2[0], d_far2[0], d_near2]).astype(BF), links.against, down_grad)
        h1 = total_of([d1[0], d_far1[0], d_near1, home2]).astype(BF)
        home1 = send("home1", h1, links.against, got_part)
        d_near0 = send("d_near0", add(d0[1], after(d_far0, h1)[1]), first)
        m2 = add(after(done[2][0], h1), swaps[2][1, ..., :width])
        m_far2 = send("m_far2", m2[2:], second, d_far0)
        parts = [d0[0], d_far0[0], d_near0, home3, home1]
        before = (home1,)
    else:
        before = ()
    got_down = give_back(down_grad, got_part, *before)
    got_full = give_back(full_grad, got_down)

    routes_mine = lax.dynamic_slice_in_dim(routes, links.t * own_rows, own_rows, 0)
    residual_grad, branch_grad, second_gain, router_part = residual_gradient(
        parts, normed_second, residual, norm_gains[1:2], router_pad, routes_mine, cotangent
    )
    branch_group = links.gather_plane(branch_grad)
    if fast:
        m1 = add(after(done[1][0], branch_grad), swaps[1][1, ..., :width])
        m_far1 = send("m_far1", m1[2:], second, branch_grad)
        m_near2 = send("m_near2", add(m2[1], after(m_far2, branch_grad)[1]), first)
        m_home2 = send("m_home2", total_of([m2[0], m_far2[0], m_near2]).astype(BF), links.against, branch_grad)
        m3 = add(after(done[3][0], branch_grad), swaps[3][1, ..., :width])
        m_far3 = send("m_far3", m3[2:], second, branch_group)
        before = (m3, got_down)
    else:
        before = ()
    dn1, attention_grad, first_gain = attend_backward(
        heads, after(info, *before), branch_group, normed_group, attention_weights, cosine, sine, qkv, attended, lse, seqs
    )
    attention_mine = lax.psum_scatter(attention_grad, "dp", scatter_dimension=0, tiled=True).astype(F32)
    n_parts = links.scatter_plane(dn1, *([m_far3, m_far1] if fast else []))
    first_grad = total_of(n_parts)
    small = jnp.concatenate([router_part, first_gain / norm_gains[0:1], second_gain])
    small = jnp.pad(small, ((0, 6), (0, 0)))
    if fast:
        m_near1 = send("m_near1", add(m1[1], m_far1[1]), first, n_parts[1])
        m0 = add(after(done[0][0], n_parts[1]), swaps[0][1, ..., :width])
        m_far0 = send("m_far0", m0[2:], second)
        m_near3 = send("m_near3", add(m3[1], m_far3[1]), first, n_parts[1], got_full)
        m_near0 = send("m_near0", add(m0[1], m_far0[1]), first, attention_mine)
        m_home3 = send("m_home3", total_of([m3[0], m_far3[0], m_near3]).astype(BF), links.along)
        m_home1 = send("m_home1", total_of([m1[0], m_far1[0], m_near1, m_home2]).astype(BF), links.against)
        out = [m0[0], m_far0[0], m_near0, m_home1, m_home3]
        before = (m_near0, m_near3)
    else:
        out = links.scatter_group([(d[0], d[2][1, ..., :width]) for d in done])
    expert_in_grad, expert_out_grad = unpack_experts(after(got_full, *before), got_down, got_part, experts, group)
    small = links.sum_all(small, *([n_parts[2], m_home1] if fast else []))
    layer_output = (residual + total_of(out)).astype(BF)

    unit = rms_unit(inputs)
    inner = first_grad * norm_gains[0]
    inverse = lax.rsqrt(jnp.mean(inputs * inputs, axis=-1, keepdims=True) + EPS)
    input_grad = residual_grad + inverse * (inner - unit * jnp.mean(inner * unit, axis=-1, keepdims=True))

    q_wide, kv_wide = heads * GRP * HD, heads * HD
    split = lambda at, size: attention_mine[:, at : at + size].reshape(depth, heads, -1)
    qkv_grad = jnp.transpose(
        jnp.concatenate(
            [split(0, q_wide), split(q_wide, kv_wide), split(q_wide + kv_wide, kv_wide)], axis=2
        ),
        (1, 0, 2),
    )
    out_weight_grad = jnp.transpose(split(q_wide + 2 * kv_wide, q_wide), (1, 2, 0))
    return (
        layer_output,
        input_grad,
        small[E : E + 2],
        jnp.transpose(small[:E]),
        qkv_grad,
        out_weight_grad,
        expert_in_grad,
        jnp.swapaxes(expert_out_grad, 1, 2),
    )


def solution(mesh):
    rows = P(("dp", "tensor"), None)
    return jax.shard_map(
        shards,
        mesh=mesh,
        in_specs=(
            rows,
            rows,
            P("dp", None),
            P("dp", None),
            P(),
            P(),
            P("tensor", "dp", None),
            P("tensor", None, "dp"),
            P("tensor", "dp", None),
            P("tensor", None, "dp"),
        ),
        out_specs=(
            rows,
            rows,
            P(),
            P(),
            P("tensor", "dp", None),
            P("tensor", None, "dp"),
            P("tensor", "dp", None),
            P("tensor", None, "dp"),
        ),
        check_vma=False,
    )
```
